32 devices in a mesh: rt: 8 (over z, y), mob: 4 (over x, core).
Axes of the slice: x: 2, y: 2, z: 4, core: 2. Of those that a mesh axis runs over, the one named last changes fastest.
Arguments:
- observed: float32 [256, 64, 1280], P('rt', 'mob'), as said below
- frame_kernel: float32 [31], replicated, may hold values from 0.05 to 1
- scan_kernel: float32 [15], replicated, may hold values from 0.05 to 1
- prec_window: int32 [256], P('rt'), may hold values from 0 to 15
- frag_window: int32 [1024], P('mob'), may hold values from 0 to 15
Outputs:
- estimate: float32 [256, 64, 1280], P('rt', 'mob')
- correlation: float32 [256, 1024], P('rt', 'mob')
The draws below stay inside these ranges and needn't reach their ends.
Inputs may be any that keep to these rules, and one draw needn't show every extreme that they name: `observed`: positive intensities.
All inputs are finite; a program needn't handle non-finite values.
Results may differ from the reference program's by a relative error of at most 0.0003.
Values sent between devices are 32-bit elements; how exact they have to be, the bound alone decides.
A program may use at most 64 MiB of HBM per device.

```python
import math
import jax
import jax.numpy as jnp
from jax import lax

PREC = 256
FRAG = 1024
KR = 31
KS = 15
ITERS = 2
WINDOWS = 16
F_DEV = 32
NF = 256
NS = 64


def draw_observed(key, part):
    keys = jax.random.split(key, 3)
    channels = PREC + FRAG
    frames = jnp.arange(NF, dtype=jnp.float32)[:, None, None]
    center = jax.random.uniform(keys[0], (1, 1, channels), jnp.float32) * NF
    sigma = 2.0 * F_DEV
    peak = jnp.exp(-0.5 * ((frames - center) / sigma) ** 2)
    ramp = 1.0 + 2.0 * frames / NF
    noise = jnp.exp(jax.random.uniform(keys[1], (NF, NS, channels), jnp.float32, math.log(0.3), math.log(3.0)))
    scale = jnp.exp(jax.random.uniform(keys[2], (1, 1, channels), jnp.float32, math.log(0.5), math.log(4.0)))
    shape_part = 0.3 + 3.0 * peak
    return (scale * ramp * shape_part * noise).astype(jnp.float32)


def with_ends(entries, own_key, smallest, largest):
    index_at = [jax.random.randint(jax.random.fold_in(own_key, axis), (), 0, length) for axis, length in enumerate(entries.shape)]
    widest = entries.shape.index(max(entries.shape))
    next_to = index_at[:widest] + [(index_at[widest] + 1) % entries.shape[widest]] + index_at[widest + 1:]
    return entries.at[tuple(index_at)].set(smallest).at[tuple(next_to)].set(largest)


def setup_inputs(seed: int = 0) -> dict:
    streams_of = jax.random.split(jax.random.key(seed), 6)
    observed = draw_observed(jax.random.fold_in(streams_of[5], 71), 0)
    frame_kernel = jnp.clip(jnp.exp(jax.random.uniform(streams_of[1], (KR,), jnp.float32, math.log(0.05), math.log(1.0))), 0.05, 1.0)
    scan_kernel = jnp.clip(jnp.exp(jax.random.uniform(streams_of[2], (KS,), jnp.float32, math.log(0.05), math.log(1.0))), 0.05, 1.0)
    prec_window = with_ends(jax.random.randint(streams_of[3], (PREC,), 0, WINDOWS), jax.random.fold_in(streams_of[3], 1), 0, WINDOWS - 1).astype(jnp.int32)
    frag_window = with_ends(jax.random.randint(streams_of[4], (FRAG,), 0, WINDOWS), jax.random.fold_in(streams_of[4], 1), 0, WINDOWS - 1).astype(jnp.int32)
    return dict(observed=observed, frame_kernel=frame_kernel, scan_kernel=scan_kernel, prec_window=prec_window, frag_window=frag_window)


def blur_along(values, kernel, along):
    radius = (kernel.shape[0] - 1) // 2
    length = values.shape[along]
    widths = [(0, 0), (0, 0), (0, 0)]
    widths[along] = (radius, radius)
    padded = jnp.pad(values, widths)
    running = kernel[0] * lax.slice_in_dim(padded, 0, length, axis=along)
    for tap_index in range(1, kernel.shape[0]):
        running = running + kernel[tap_index] * lax.slice_in_dim(padded, tap_index, tap_index + length, axis=along)
    return running

def forward_blur(values, frame_kernel, scan_kernel):
    return blur_along(blur_along(values, scan_kernel, 1), frame_kernel, 0)

def adjoint_blur(values, frame_kernel, scan_kernel):
    return blur_along(blur_along(values, frame_kernel[::-1], 0), scan_kernel[::-1], 1)

def reference(observed, frame_kernel, scan_kernel, prec_window, frag_window):
    estimate = observed
    for iteration in range(ITERS):
        ratio_field = observed / forward_blur(estimate, frame_kernel, scan_kernel)
        estimate = estimate * adjoint_blur(ratio_field, frame_kernel, scan_kernel)
    profiles = estimate.reshape(NF * NS, PREC + FRAG)
    channel_mean = lax.optimization_barrier(jnp.sum(profiles, axis=0)) / (NF * NS)
    centered = (profiles - channel_mean).astype(jnp.bfloat16)
    as_float = centered.astype(jnp.float32)
    squares = lax.optimization_barrier(jnp.sum(as_float * as_float, axis=0))
    cross_sums = lax.dot_general(centered[:, :PREC], centered[:, PREC:], (((0,), (0,)), ((), ())), preferred_element_type=jnp.float32)
    inverse_norm = 1.0 / jnp.sqrt(squares + 1e-06)
    pair_mask = (prec_window[:, None] == frag_window[None, :]).astype(jnp.float32)
    correlation = pair_mask * cross_sums * inverse_norm[:PREC][:, None] * inverse_norm[PREC:][None, :]
    return (estimate, correlation)
```

```python
import functools

import jax
import jax.numpy as jnp
from jax import lax
from jax.experimental import pallas as pl
from jax.experimental.pallas import tpu as pltpu
from jax.sharding import PartitionSpec as P

PREC = 256
ITERS = 2
LANES = 128
SUB = 8
STEP = 16


def scan_taps(pad_ref, frame, taps, scans):
    radius = (len(taps) - 1) // 2
    total = None
    for a, tap in enumerate(taps):
        part = tap * pad_ref[frame, pl.ds(SUB - radius + a, scans), :]
        total = part if total is None else total + part
    return total


def scan_kernel_body(flip, k_ref, mid_ref, lo_ref, hi_ref, *rest):
    *scale, out_ref, pad_ref = rest
    frames, scans, _ = mid_ref.shape
    count = k_ref.shape[0]
    taps = [k_ref[count - 1 - a if flip else a] for a in range(count)]
    pad_ref[:, :SUB, :] = lo_ref[...]
    pad_ref[:, SUB : SUB + scans, :] = mid_ref[...]
    pad_ref[:, SUB + scans :, :] = hi_ref[...]

    def one(frame, carry):
        total = scan_taps(pad_ref, frame, taps, scans)
        if scale:
            total = scale[0][frame] * total
        out_ref[frame] = total
        return carry

    lax.fori_loop(0, frames, one, 0, unroll=4)


def frame_kernel_body(flip, divide, k_ref, mid_ref, lo_ref, hi_ref, *rest):
    *above, out_ref, pad_ref = rest
    frames, scans, _ = mid_ref.shape
    count = k_ref.shape[0]
    radius = (count - 1) // 2
    pad_ref[:radius] = lo_ref[...]
    pad_ref[radius : radius + frames] = mid_ref[...]
    pad_ref[radius + frames :] = hi_ref[...]
    taps = [
        jnp.full((SUB, LANES), k_ref[count - 1 - a if flip else a], jnp.float32)
        for a in range(count)
    ]
    rows_of = scans // SUB

    def block(index, carry):
        first = (index // rows_of) * STEP
        rows = pl.ds(pl.multiple_of((index % rows_of) * SUB, SUB), SUB)
        totals = [None] * STEP
        for j in range(STEP + count - 1):
            value = pad_ref[first + j, rows, :]
            for i in range(STEP):
                if 0 <= j - i < count:
                    part = taps[j - i] * value
                    totals[i] = part if totals[i] is None else totals[i] + part
        for i in range(STEP):
            result = totals[i]
            if divide:
                result = above[0][first + i, rows, :] / result
            out_ref[first + i, rows, :] = result
        return carry

    lax.fori_loop(0, (frames // STEP) * rows_of, block, 0)


def blur(body, taps, arrays, pad_shape):
    frames, scans, channels = arrays[0].shape

    def spec(array):
        return pl.BlockSpec((array.shape[0], array.shape[1], LANES), lambda c: (0, 0, c))

    return pl.pallas_call(
        body,
        grid=(channels // LANES,),
        in_specs=[pl.BlockSpec(memory_space=pltpu.SMEM)] + [spec(a) for a in arrays],
        out_specs=pl.BlockSpec((frames, scans, LANES), lambda c: (0, 0, c)),
        out_shape=jax.ShapeDtypeStruct((frames, scans, channels), jnp.float32),
        scratch_shapes=[pltpu.VMEM(pad_shape, jnp.float32)],
        compiler_params=pltpu.CompilerParams(vmem_limit_bytes=32 * 1024 * 1024),
        cost_estimate=pl.CostEstimate(
            flops=2 * taps.shape[0] * frames * scans * channels,
            bytes_accessed=12 * frames * scans * channels,
            transcendentals=0,
        ),
    )(taps, *arrays)


def halo(cells, axis, dim, width, hop):
    count = lax.axis_size(axis)
    size = cells.shape[dim]
    up = [(i, i + hop) for i in range(count - hop)]
    down = [(i + hop, i) for i in range(count - hop)]
    before = lax.ppermute(lax.slice_in_dim(cells, size - width, size, axis=dim), axis, up)
    after = lax.ppermute(lax.slice_in_dim(cells, 0, width, axis=dim), axis, down)
    return before, after


def local(observed, frame_kernel, scan_kernel, prec_window, frag_window):
    frames, scan_count, channels = observed.shape
    radius = (frame_kernel.shape[0] - 1) // 2
    half = channels // 2
    count = lax.axis_size("rt")
    side = lax.rem(lax.axis_index("rt"), 2)
    swap = [(i, i ^ 1) for i in range(count)]

    def blur_scans(flip, cells, *scale):
        before, after = halo(cells, "mob", 1, SUB, 1)
        return blur(
            functools.partial(scan_kernel_body, flip),
            scan_kernel,
            (cells, before, after) + scale,
            (cells.shape[0], scan_count + 2 * SUB, LANES),
        )

    def blur_frames(flip, cells, *above):
        before, after = halo(cells, "rt", 0, radius, 2)
        return blur(
            functools.partial(frame_kernel_body, flip, bool(above)),
            frame_kernel,
            (cells, before, after) + above,
            (cells.shape[0] + 2 * radius, scan_count, LANES),
        )

    mine = lax.dynamic_slice_in_dim(observed, side * half, half, axis=2)
    other = lax.dynamic_slice_in_dim(observed, (1 - side) * half, half, axis=2)
    other = lax.ppermute(other, "rt", swap)
    first = side == 0
    wide = jnp.concatenate([jnp.where(first, mine, other), jnp.where(first, other, mine)], axis=0)
    estimate = wide
    for iteration in range(ITERS):
        ratio = blur_frames(False, blur_scans(False, estimate), wide)
        estimate = blur_scans(True, blur_frames(True, ratio), estimate)
    mine = lax.dynamic_slice_in_dim(estimate, side * frames, frames, axis=0)
    other = lax.dynamic_slice_in_dim(estimate, (1 - side) * frames, frames, axis=0)
    other = lax.ppermute(other, "rt", swap)
    estimate = jnp.concatenate(
        [jnp.where(first, mine, other), jnp.where(first, other, mine)], axis=2
    )
    profiles = estimate.reshape(frames * scan_count, channels)
    cell_count = frames * scan_count * lax.axis_size("rt") * lax.axis_size("mob")
    channel_total = lax.psum(jnp.sum(profiles, axis=0), ("rt", "mob"))
    channel_mean = channel_total / cell_count
    centered = (profiles - channel_mean).astype(jnp.bfloat16)
    as_float = centered.astype(jnp.float32)
    squares = lax.psum(jnp.sum(as_float * as_float, axis=0), ("rt", "mob"))
    cross_sums = lax.dot_general(
        centered[:, :PREC],
        centered[:, PREC:],
        (((0,), (0,)), ((), ())),
        preferred_element_type=jnp.float32,
    )
    partial_value = lax.psum_scatter(cross_sums, "mob", scatter_dimension=1, tiled=True)
    block_sums = lax.psum_scatter(partial_value, "rt", scatter_dimension=0, tiled=True)
    row_count = prec_window.shape[0]
    column_count = frag_window.shape[0]
    inverse_norm = 1.0 / jnp.sqrt(squares + 1e-06)
    row_inverse = lax.dynamic_slice_in_dim(
        inverse_norm[:PREC], lax.axis_index("rt") * row_count, row_count
    )
    column_inverse = lax.dynamic_slice_in_dim(
        inverse_norm[PREC:], lax.axis_index("mob") * column_count, column_count
    )
    pair_mask = (prec_window[:, None] == frag_window[None, :]).astype(jnp.float32)
    correlation = pair_mask * block_sums * row_inverse[:, None] * column_inverse[None, :]
    return (estimate, correlation)


def solution(mesh):
    placed = (P("rt", "mob", None), P(), P(), P("rt"), P("mob"))
    return jax.shard_map(
        local,
        mesh=mesh,
        in_specs=placed,
        out_specs=(P("rt", "mob", None), P("rt", "mob")),
        check_vma=False,
    )
```

```python
import functools

import jax
import jax.numpy as jnp
from jax import lax
from jax.experimental import pallas as pl
from jax.experimental.pallas import tpu as pltpu
from jax.sharding import PartitionSpec as P

PREC = 256
ITERS = 2
LANES = 128
SUB = 8
STEP = 16


def scan_taps(pad_ref, frame, taps, scans):
    radius = (len(taps) - 1) // 2
    total = None
    for a, tap in enumerate(taps):
        part = tap * pad_ref[frame, pl.ds(SUB - radius + a, scans), :]
        total = part if total is None else total + part
    return total


def scan_kernel_body(flip, k_ref, mid_ref, lo_ref, hi_ref, *rest):
    *scale, out_ref, pad_ref = rest
    frames, scans, _ = mid_ref.shape
    count = k_ref.shape[0]
    taps = [k_ref[count - 1 - a if flip else a] for a in range(count)]
    pad_ref[:, :SUB, :] = lo_ref[...]
    pad_ref[:, SUB : SUB + scans, :] = mid_ref[...]
    pad_ref[:, SUB + scans :, :] = hi_ref[...]

    def one(frame, carry):
        total = scan_taps(pad_ref, frame, taps, scans)
        if scale:
            total = scale[0][frame] * total
        out_ref[frame] = total
        return carry

    lax.fori_loop(0, frames, one, 0, unroll=4)


def frame_kernel_body(flip, divide, k_ref, mid_ref, lo_ref, hi_ref, *rest):
    *above, out_ref, pad_ref = rest
    frames, scans, _ = mid_ref.shape
    count = k_ref.shape[0]
    radius = (count - 1) // 2
    pad_ref[:radius] = lo_ref[...]
    pad_ref[radius : radius + frames] = mid_ref[...]
    pad_ref[radius + frames :] = hi_ref[...]
    taps = [
        jnp.full((SUB, LANES), k_ref[count - 1 - a if flip else a], jnp.float32)
        for a in range(count)
    ]
    rows_of = scans // SUB

    def block(index, carry):
        first = (index // rows_of) * STEP
        rows = pl.ds(pl.multiple_of((index % rows_of) * SUB, SUB), SUB)
        totals = [None] * STEP
        for j in range(STEP + count - 1):
            value = pad_ref[first + j, rows, :]
            for i in range(STEP):
                if 0 <= j - i < count:
                    part = taps[j - i] * value
                    totals[i] = part if totals[i] is None else totals[i] + part
        for i in range(STEP):
            result = totals[i]
            if divide:
                result = above[0][first + i, rows, :] / result
            out_ref[first + i, rows, :] = result
        return carry

    lax.fori_loop(0, (frames // STEP) * rows_of, block, 0)


def blur(body, taps, arrays, pad_shape):
    frames, scans, channels = arrays[0].shape

    def spec(array):
        return pl.BlockSpec((array.shape[0], array.shape[1], LANES), lambda c: (0, 0, c))

    return pl.pallas_call(
        body,
        grid=(channels // LANES,),
        in_specs=[pl.BlockSpec(memory_space=pltpu.SMEM)] + [spec(a) for a in arrays],
        out_specs=pl.BlockSpec((frames, scans, LANES), lambda c: (0, 0, c)),
        out_shape=jax.ShapeDtypeStruct((frames, scans, channels), jnp.float32),
        scratch_shapes=[pltpu.VMEM(pad_shape, jnp.float32)],
        compiler_params=pltpu.CompilerParams(vmem_limit_bytes=32 * 1024 * 1024),
        cost_estimate=pl.CostEstimate(
            flops=2 * taps.shape[0] * frames * scans * channels,
            bytes_accessed=12 * frames * scans * channels,
            transcendentals=0,
        ),
    )(taps, *arrays)


def halo(cells, axis, dim, width, hop):
    count = lax.axis_size(axis)
    size = cells.shape[dim]
    up = [(i, i + hop) for i in range(count - hop)]
    down = [(i + hop, i) for i in range(count - hop)]
    before = lax.ppermute(lax.slice_in_dim(cells, size - width, size, axis=dim), axis, up)
    after = lax.ppermute(lax.slice_in_dim(cells, 0, width, axis=dim), axis, down)
    return before, after


def partner(axis, bit):
    return lax.bitwise_xor(lax.axis_index(axis), bit)


def bits_of(size):
    return [1 << n for n in range(size.bit_length() - 1)]


def greet(stages):
    barrier = pltpu.get_barrier_semaphore()
    for axis, bit in stages:
        pl.semaphore_signal(
            barrier,
            inc=1,
            device_id={axis: partner(axis, bit)},
            device_id_type=pl.DeviceIdType.MESH,
        )
    pl.semaphore_wait(barrier, len(stages))


def exchange(src, dst, send_sem, recv_sem, stage):
    axis, bit = stage
    copy = pltpu.make_async_remote_copy(
        src_ref=src,
        dst_ref=dst,
        send_sem=send_sem,
        recv_sem=recv_sem,
        device_id={axis: partner(axis, bit)},
        device_id_type=pl.DeviceIdType.MESH,
    )
    copy.start()
    return copy


def correlate_body(stages, groups, cells, est_ref, prow_ref, fcol_ref, out_ref, *scratch):
    count = len(stages)
    sums, got, sum_send, sum_recv, send_sem, recv_sem = scratch[:6]
    held = scratch[6 : 6 + count]
    landed = scratch[6 + count :]
    mobs, rows_of = groups
    prec = est_ref.shape[1] - mobs * out_ref.shape[1]
    rows, columns = out_ref.shape
    greet(stages)
    sums[0] = jnp.broadcast_to(
        jnp.sum(est_ref[...], axis=0, keepdims=True), sums.shape[1:]
    )
    for n, stage in enumerate(stages):
        copy = exchange(sums.at[n], got.at[n], sum_send.at[n], sum_recv.at[n], stage)
        copy.wait()
        sums[n + 1] = sums[n] + got[n]
    mean = sums[count, :1, :] / cells
    left = (est_ref[:, :prec] - mean[:, :prec]).astype(jnp.bfloat16)
    wide = left.astype(jnp.float32)
    left_squares = jnp.sum(wide * wide, axis=0, keepdims=True)
    across = left.T
    first = held[0]
    for m in range(mobs):
        start = prec + m * columns
        right = (
            est_ref[:, start : start + columns] - mean[:, start : start + columns]
        ).astype(jnp.bfloat16)
        wide = right.astype(jnp.float32)
        right_squares = jnp.sum(wide * wide, axis=0, keepdims=True)
        product = jnp.dot(across, right, preferred_element_type=jnp.float32)
        for r in range(rows_of):
            block = first.at[m // 2, m % 2, r]
            block[:rows, :] = product[r * rows : (r + 1) * rows, :]
            block[rows : rows + 8, :] = jnp.broadcast_to(right_squares, (8, columns))
            block[rows + 8 :, :] = jnp.broadcast_to(left_squares, (8, prec))
    for n, stage in enumerate(stages):
        axis, bit = stage
        mine = lax.rem(lax.axis_index(axis) // bit, 2)
        copy = exchange(
            held[n].at[:, 1 - mine], landed[n], send_sem.at[n], recv_sem.at[n], stage
        )
        copy.wait()
        span = held[n].shape[0]
        for i in range(span):
            total = held[n][i, mine] + landed[n][i]
            if n + 1 == count:
                column = 1.0 / jnp.sqrt(total[rows : rows + 1, :] + 1e-06)
                row = 1.0 / jnp.sqrt(total[rows + 8 : rows + 9, :] + 1e-06)
                place = lax.broadcasted_iota(jnp.int32, (rows, prec), 1)
                wanted = lax.broadcasted_iota(jnp.int32, (rows, prec), 0)
                wanted = wanted + lax.axis_index("rt") * rows
                row = jnp.sum(jnp.where(place == wanted, row, 0.0), axis=1, keepdims=True)
                same = (prow_ref[...] == fcol_ref[...]).astype(jnp.float32)
                out_ref[...] = same * total[:rows, :] * row * column
            elif stages[n + 1][0] == axis:
                held[n + 1][i // 2, i % 2] = total
            else:
                for r in range(rows_of):
                    held[n + 1][r // 2, r % 2] = total[r]


def correlate(estimate, prec_window, frag_window):
    frames, scans, channels = estimate.shape
    mobs, rows_of = lax.axis_size("mob"), lax.axis_size("rt")
    rows, columns = prec_window.shape[0], frag_window.shape[0]
    stages = [("mob", bit) for bit in bits_of(mobs)] + [("rt", bit) for bit in bits_of(rows_of)]
    count = len(stages)
    tile = (rows + 16, columns)
    held, landed = [], []
    for axis, bit in stages:
        if axis == "mob":
            span, tail = mobs // (2 * bit), (rows_of,) + tile
        else:
            span, tail = rows_of // (2 * bit), tile
        held.append(pltpu.VMEM((span, 2) + tail, jnp.float32))
        landed.append(pltpu.VMEM((span,) + tail, jnp.float32))
    whole = pl.BlockSpec(memory_space=pltpu.VMEM)
    cells = frames * scans * mobs * rows_of
    return pl.pallas_call(
        functools.partial(correlate_body, stages, (mobs, rows_of), cells),
        in_specs=[whole] * 3,
        out_specs=whole,
        out_shape=jax.ShapeDtypeStruct((rows, columns), jnp.float32),
        scratch_shapes=[
            pltpu.VMEM((count + 1, SUB, channels), jnp.float32),
            pltpu.VMEM((count, SUB, channels), jnp.float32),
            pltpu.SemaphoreType.DMA((count,)),
            pltpu.SemaphoreType.DMA((count,)),
            pltpu.SemaphoreType.DMA((count,)),
            pltpu.SemaphoreType.DMA((count,)),
        ]
        + held
        + landed,
        compiler_params=pltpu.CompilerParams(
            collective_id=1, has_side_effects=True, vmem_limit_bytes=40 * 1024 * 1024
        ),
        cost_estimate=pl.CostEstimate(
            flops=2 * frames * scans * PREC * (channels - PREC),
            bytes_accessed=4 * frames * scans * channels,
            transcendentals=0,
        ),
    )(
        estimate.reshape(frames * scans, channels),
        prec_window.reshape(rows, 1),
        frag_window.reshape(1, columns),
    )


def local(observed, frame_kernel, scan_kernel, prec_window, frag_window):
    frames, scan_count, channels = observed.shape
    radius = (frame_kernel.shape[0] - 1) // 2
    half = channels // 2
    count = lax.axis_size("rt")
    side = lax.rem(lax.axis_index("rt"), 2)
    swap = [(i, i ^ 1) for i in range(count)]

    def blur_scans(flip, cells, *scale):
        before, after = halo(cells, "mob", 1, SUB, 1)
        return blur(
            functools.partial(scan_kernel_body, flip),
            scan_kernel,
            (cells, before, after) + scale,
            (cells.shape[0], scan_count + 2 * SUB, LANES),
        )

    def blur_frames(flip, cells, *above):
        before, after = halo(cells, "rt", 0, radius, 2)
        return blur(
            functools.partial(frame_kernel_body, flip, bool(above)),
            frame_kernel,
            (cells, before, after) + above,
            (cells.shape[0] + 2 * radius, scan_count, LANES),
        )

    mine = lax.dynamic_slice_in_dim(observed, side * half, half, axis=2)
    other = lax.dynamic_slice_in_dim(observed, (1 - side) * half, half, axis=2)
    other = lax.ppermute(other, "rt", swap)
    first = side == 0
    wide = jnp.concatenate([jnp.where(first, mine, other), jnp.where(first, other, mine)], axis=0)
    estimate = wide
    for iteration in range(ITERS):
        ratio = blur_frames(False, blur_scans(False, estimate), wide)
        estimate = blur_scans(True, blur_frames(True, ratio), estimate)
    mine = lax.dynamic_slice_in_dim(estimate, side * frames, frames, axis=0)
    other = lax.dynamic_slice_in_dim(estimate, (1 - side) * frames, frames, axis=0)
    other = lax.ppermute(other, "rt", swap)
    estimate = jnp.concatenate(
        [jnp.where(first, mine, other), jnp.where(first, other, mine)], axis=2
    )
    return (estimate, correlate(estimate, prec_window, frag_window))


def solution(mesh):
    placed = (P("rt", "mob", None), P(), P(), P("rt"), P("mob"))
    return jax.shard_map(
        local,
        mesh=mesh,
        in_specs=placed,
        out_specs=(P("rt", "mob", None), P("rt", "mob")),
        check_vma=False,
    )
```

```python
import functools

import jax
import jax.numpy as jnp
from jax import lax
from jax.experimental import pallas as pl
from jax.experimental.pallas import tpu as pltpu
from jax.sharding import PartitionSpec as P

PREC = 256
ITERS = 2
LANES = 128
SUB = 8
STEP = 16


def flipped(k_ref, flip):
    count = k_ref.shape[0]
    return [k_ref[count - 1 - a if flip else a] for a in range(count)]


def blur_scans(taps, src, scans, emit):
    radius = (len(taps) - 1) // 2

    def one(frame, carry):
        total = None
        for a, tap in enumerate(taps):
            part = tap * src[frame, pl.ds(SUB - radius + a, scans), :]
            total = part if total is None else total + part
        emit(frame, total)
        return carry

    lax.fori_loop(0, src.shape[0], one, 0, unroll=4)


def blur_frames(scalars, src, frames, emit):
    count = len(scalars)
    taps = [jnp.full((SUB, LANES), tap, jnp.float32) for tap in scalars]
    rows_of = src.shape[1] // SUB

    def block(index, carry):
        first = (index // rows_of) * STEP
        start = lax.rem(index, rows_of) * SUB
        rows = pl.ds(pl.multiple_of(start, SUB), SUB)
        totals = [None] * STEP
        for j in range(STEP + count - 1):
            value = src[first + j, rows, :]
            for i in range(STEP):
                if 0 <= j - i < count:
                    part = taps[j - i] * value
                    totals[i] = part if totals[i] is None else totals[i] + part
        for i in range(STEP):
            emit(first + i, start, totals[i])
        return carry

    lax.fori_loop(0, (frames // STEP) * rows_of, block, 0)


def deblur_body(sizes, fk_ref, sk_ref, obs_ref, out_ref, *scratch):
    est, blurred, ratio, back, send, recv, swap_send, swap_recv, own_sem = scratch
    rt_size, mob_size = sizes
    frames, scans, channels = obs_ref.shape
    half = channels // 2
    tiles = half // LANES
    long = 2 * frames
    radius = (fk_ref.shape[0] - 1) // 2
    rt, mob = lax.axis_index("rt"), lax.axis_index("mob")
    side = lax.rem(rt, 2)
    mid = pl.ds(SUB, scans)
    has = {
        ("rt", 0): rt >= 2,
        ("rt", 1): rt < rt_size - 2,
        ("mob", 0): mob > 0,
        ("mob", 1): mob < mob_size - 1,
    }
    to = {
        ("rt", 0): lax.rem(rt + rt_size - 2, rt_size),
        ("rt", 1): lax.rem(rt + 2, rt_size),
        ("mob", 0): lax.rem(mob + mob_size - 1, mob_size),
        ("mob", 1): lax.rem(mob + 1, mob_size),
    }
    mate = lax.bitwise_xor(rt, 1)
    mesh_type = pl.DeviceIdType.MESH

    barrier = pltpu.get_barrier_semaphore()
    pl.semaphore_signal(barrier, inc=1, device_id={"rt": mate}, device_id_type=mesh_type)
    for key in has:

        @pl.when(has[key])
        def _(key=key):
            pl.semaphore_signal(
                barrier, inc=1, device_id={key[0]: to[key]}, device_id_type=mesh_type
            )

    peers = 1
    for key in has:
        peers = peers + has[key].astype(jnp.int32)
    pl.semaphore_wait(barrier, peers)

    def lanes_of(which, c):
        return pl.ds(pl.multiple_of(which * half + c * LANES, LANES), LANES)

    def landing(c):
        return est.at[0, c, pl.ds(side * frames, frames), mid, :]

    def swap_in_remote(c):
        return pltpu.make_async_remote_copy(
            src_ref=obs_ref.at[:, :, lanes_of(1 - side, c)],
            dst_ref=landing(c),
            send_sem=swap_send.at[0, c],
            recv_sem=swap_recv.at[0, c],
            device_id={"rt": mate},
            device_id_type=mesh_type,
        )

    def swap_in(c):
        own = pltpu.make_async_copy(
            obs_ref.at[:, :, lanes_of(side, c)], landing(c), own_sem.at[0, c]
        )
        return swap_in_remote(c), own

    def swap_out(c):
        away = pltpu.make_async_remote_copy(
            src_ref=est.at[ITERS, c, pl.ds((1 - side) * frames, frames), mid, :],
            dst_ref=out_ref.at[:, :, lanes_of(side, c)],
            send_sem=swap_send.at[1, c],
            recv_sem=swap_recv.at[1, c],
            device_id={"rt": mate},
            device_id_type=mesh_type,
        )
        own = pltpu.make_async_copy(
            est.at[ITERS, c, pl.ds(side * frames, frames), mid, :],
            out_ref.at[:, :, lanes_of(side, c)],
            own_sem.at[1, c],
        )
        return away, own

    def start_both(pair):
        pair[0].start()
        pair[1].start()

    fields = (est, blurred, ratio, back)

    def halo(kind, it, c, way):
        cells = fields[kind].at[it, c]
        if kind in (0, 3):
            axis = "mob"
            src = cells.at[:, pl.ds(scans if way else SUB, SUB), :]
            dst = cells.at[:, pl.ds(0 if way else SUB + scans, SUB), :]
        else:
            axis = "rt"
            src = cells.at[pl.ds(long if way else radius, radius)]
            dst = cells.at[pl.ds(0 if way else radius + long, radius)]
        return axis, pltpu.make_async_remote_copy(
            src_ref=src,
            dst_ref=dst,
            send_sem=send.at[kind, it, c, way],
            recv_sem=recv.at[kind, it, c, way],
            device_id={axis: to[axis, way]},
            device_id_type=mesh_type,
        )

    def on_halo(kind, it, c, act, flip):
        axis = "mob" if kind in (0, 3) else "rt"
        for way in (0, 1):

            @pl.when(has[axis, 1 - way if flip else way])
            def _(way=way):
                act(halo(kind, it, c, way)[1])

    def start_halo(kind, it, c):
        on_halo(kind, it, c, lambda copy: copy.start(), False)

    def wait_halo(kind, it, c):
        on_halo(kind, it, c, lambda copy: copy.wait_recv(), True)

    def begin(c, carry):
        start_both(swap_in(c))
        return carry

    lax.fori_loop(0, tiles, begin, 0)

    def clear(index, carry):
        it, c = index // tiles, lax.rem(index, tiles)
        for field in (est, back):
            for way, start in ((0, 0), (1, SUB + scans)):

                @pl.when(jnp.logical_not(has["mob", way]))
                def _(field=field, start=start):
                    field[it, c, :, pl.ds(start, SUB), :] = jnp.zeros(
                        (long, SUB, LANES), jnp.float32
                    )

        for field in (blurred, ratio):
            for way, start in ((0, 0), (1, radius + long)):

                @pl.when(jnp.logical_not(has["rt", way]))
                def _(field=field, start=start):
                    field[it, c, pl.ds(start, radius)] = jnp.zeros(
                        (radius, scans, LANES), jnp.float32
                    )

        return carry

    lax.fori_loop(0, ITERS * tiles, clear, 0)

    def arrive(c):
        away, own = swap_in(c)
        own.wait()
        away.wait_recv()
        start_halo(0, 0, c)

    def forward_scans(it, c):
        wait_halo(0, it, c)

        def emit(frame, total):
            blurred[it, c, radius + frame] = total

        blur_scans(flipped(sk_ref, False), est.at[it, c], scans, emit)
        start_halo(1, it, c)

    def forward_frames(it, c):
        wait_halo(1, it, c)

        def emit(frame, start, total):
            seen = est[0, c, frame, pl.ds(pl.multiple_of(SUB + start, SUB), SUB), :]
            ratio[it, c, radius + frame, pl.ds(pl.multiple_of(start, SUB), SUB), :] = seen / total

        blur_frames(flipped(fk_ref, False), blurred.at[it, c], long, emit)
        start_halo(2, it, c)

    def back_frames(it, c):
        wait_halo(2, it, c)

        def emit(frame, start, total):
            back[it, c, frame, pl.ds(pl.multiple_of(SUB + start, SUB), SUB), :] = total

        blur_frames(flipped(fk_ref, True), ratio.at[it, c], long, emit)
        start_halo(3, it, c)

    def back_scans(it, c):
        wait_halo(3, it, c)

        def emit(frame, total):
            est[it + 1, c, frame, mid, :] = est[it, c, frame, mid, :] * total

        blur_scans(flipped(sk_ref, True), back.at[it, c], scans, emit)

        @pl.when(it < ITERS - 1)
        def _():
            start_halo(0, it + 1, c)

        @pl.when(it == ITERS - 1)
        def _():
            start_both(swap_out(c))

    steps = (forward_scans, forward_frames, back_frames, back_scans)
    total_steps = len(steps) * ITERS
    arrive(0)

    def wave(t, carry):
        def tile(c, inner):
            stage = t - c
            live = jnp.logical_and(stage >= 0, stage < total_steps)
            for n, step in enumerate(steps):

                @pl.when(jnp.logical_and(live, lax.rem(stage + total_steps, len(steps)) == n))
                def _(step=step):
                    step(stage // len(steps), c)

            return inner

        lax.fori_loop(0, tiles, tile, 0)

        @pl.when(t + 1 < tiles)
        def _():
            arrive(t + 1)

        return carry

    lax.fori_loop(0, total_steps + tiles - 1, wave, 0)

    def finish(c, carry):
        away, own = swap_out(c)
        own.wait()
        away.wait()
        swap_in_remote(c).wait_send()
        return carry

    lax.fori_loop(0, tiles, finish, 0)

    def sent(index, carry):
        it, c = index // tiles, lax.rem(index, tiles)
        for kind in range(len(fields)):
            on_halo(kind, it, c, lambda copy: copy.wait_send(), False)
        return carry

    lax.fori_loop(0, ITERS * tiles, sent, 0)


def deblur(observed, frame_kernel, scan_kernel):
    frames, scans, channels = observed.shape
    tiles = channels // 2 // LANES
    radius = (frame_kernel.shape[0] - 1) // 2
    sizes = lax.axis_size("rt"), lax.axis_size("mob")
    tall = (2 * frames, scans + 2 * SUB, LANES)
    long = (2 * frames + 2 * radius, scans, LANES)
    smem = pl.BlockSpec(memory_space=pltpu.SMEM)
    anywhere = pl.BlockSpec(memory_space=pl.ANY)
    dma = pltpu.SemaphoreType.DMA
    return pl.pallas_call(
        functools.partial(deblur_body, sizes),
        in_specs=[smem, smem, anywhere],
        out_specs=anywhere,
        out_shape=jax.ShapeDtypeStruct(observed.shape, jnp.float32),
        scratch_shapes=[
            pltpu.VMEM((ITERS + 1, tiles) + tall, jnp.float32),
            pltpu.VMEM((ITERS, tiles) + long, jnp.float32),
            pltpu.VMEM((ITERS, tiles) + long, jnp.float32),
            pltpu.VMEM((ITERS, tiles) + tall, jnp.float32),
            dma((4, ITERS, tiles, 2)),
            dma((4, ITERS, tiles, 2)),
            dma((2, tiles)),
            dma((2, tiles)),
            dma((2, tiles)),
        ],
        compiler_params=pltpu.CompilerParams(
            collective_id=2, has_side_effects=True, vmem_limit_bytes=50 * 1024 * 1024
        ),
        cost_estimate=pl.CostEstimate(
            flops=4 * ITERS * (frame_kernel.shape[0] + scan_kernel.shape[0]) * observed.size,
            bytes_accessed=8 * observed.size,
            transcendentals=0,
        ),
    )(frame_kernel, scan_kernel, observed)


def partner(axis, bit):
    return lax.bitwise_xor(lax.axis_index(axis), bit)


def bits_of(size):
    return [1 << n for n in range(size.bit_length() - 1)]


def greet(stages):
    barrier = pltpu.get_barrier_semaphore()
    for axis, bit in stages:
        pl.semaphore_signal(
            barrier,
            inc=1,
            device_id={axis: partner(axis, bit)},
            device_id_type=pl.DeviceIdType.MESH,
        )
    pl.semaphore_wait(barrier, len(stages))


def exchange(src, dst, send_sem, recv_sem, stage):
    axis, bit = stage
    copy = pltpu.make_async_remote_copy(
        src_ref=src,
        dst_ref=dst,
        send_sem=send_sem,
        recv_sem=recv_sem,
        device_id={axis: partner(axis, bit)},
        device_id_type=pl.DeviceIdType.MESH,
    )
    copy.start()
    return copy


def correlate_body(stages, groups, cells, est_ref, prow_ref, fcol_ref, out_ref, *scratch):
    count = len(stages)
    sums, got, sum_send, sum_recv, send_sem, recv_sem = scratch[:6]
    held = scratch[6 : 6 + count]
    landed = scratch[6 + count :]
    mobs, rows_of = groups
    prec = est_ref.shape[1] - mobs * out_ref.shape[1]
    rows, columns = out_ref.shape
    greet(stages)
    sums[0] = jnp.broadcast_to(
        jnp.sum(est_ref[...], axis=0, keepdims=True), sums.shape[1:]
    )
    for n, stage in enumerate(stages):
        copy = exchange(sums.at[n], got.at[n], sum_send.at[n], sum_recv.at[n], stage)
        copy.wait()
        sums[n + 1] = sums[n] + got[n]
    mean = sums[count, :1, :] / cells
    left = (est_ref[:, :prec] - mean[:, :prec]).astype(jnp.bfloat16)
    wide = left.astype(jnp.float32)
    left_squares = jnp.sum(wide * wide, axis=0, keepdims=True)
    across = left.T
    first = held[0]
    for m in range(mobs):
        start = prec + m * columns
        right = (
            est_ref[:, start : start + columns] - mean[:, start : start + columns]
        ).astype(jnp.bfloat16)
        wide = right.astype(jnp.float32)
        right_squares = jnp.sum(wide * wide, axis=0, keepdims=True)
        product = jnp.dot(across, right, preferred_element_type=jnp.float32)
        for r in range(rows_of):
            block = first.at[m // 2, m % 2, r]
            block[:rows, :] = product[r * rows : (r + 1) * rows, :]
            block[rows : rows + 8, :] = jnp.broadcast_to(right_squares, (8, columns))
            block[rows + 8 :, :] = jnp.broadcast_to(left_squares, (8, prec))
    for n, stage in enumerate(stages):
        axis, bit = stage
        mine = lax.rem(lax.axis_index(axis) // bit, 2)
        copy = exchange(
            held[n].at[:, 1 - mine], landed[n], send_sem.at[n], recv_sem.at[n], stage
        )
        copy.wait()
        span = held[n].shape[0]
        for i in range(span):
            total = held[n][i, mine] + landed[n][i]
            if n + 1 == count:
                column = 1.0 / jnp.sqrt(total[rows : rows + 1, :] + 1e-06)
                row = 1.0 / jnp.sqrt(total[rows + 8 : rows + 9, :] + 1e-06)
                place = lax.broadcasted_iota(jnp.int32, (rows, prec), 1)
                wanted = lax.broadcasted_iota(jnp.int32, (rows, prec), 0)
                wanted = wanted + lax.axis_index("rt") * rows
                row = jnp.sum(jnp.where(place == wanted, row, 0.0), axis=1, keepdims=True)
                same = (prow_ref[...] == fcol_ref[...]).astype(jnp.float32)
                out_ref[...] = same * total[:rows, :] * row * column
            elif stages[n + 1][0] == axis:
                held[n + 1][i // 2, i % 2] = total
            else:
                for r in range(rows_of):
                    held[n + 1][r // 2, r % 2] = total[r]


def correlate(estimate, prec_window, frag_window):
    frames, scans, channels = estimate.shape
    mobs, rows_of = lax.axis_size("mob"), lax.axis_size("rt")
    rows, columns = prec_window.shape[0], frag_window.shape[0]
    stages = [("mob", bit) for bit in bits_of(mobs)] + [("rt", bit) for bit in bits_of(rows_of)]
    count = len(stages)
    tile = (rows + 16, columns)
    held, landed = [], []
    for axis, bit in stages:
        if axis == "mob":
            span, tail = mobs // (2 * bit), (rows_of,) + tile
        else:
            span, tail = rows_of // (2 * bit), tile
        held.append(pltpu.VMEM((span, 2) + tail, jnp.float32))
        landed.append(pltpu.VMEM((span,) + tail, jnp.float32))
    whole = pl.BlockSpec(memory_space=pltpu.VMEM)
    cells = frames * scans * mobs * rows_of
    return pl.pallas_call(
        functools.partial(correlate_body, stages, (mobs, rows_of), cells),
        in_specs=[whole] * 3,
        out_specs=whole,
        out_shape=jax.ShapeDtypeStruct((rows, columns), jnp.float32),
        scratch_shapes=[
            pltpu.VMEM((count + 1, SUB, channels), jnp.float32),
            pltpu.VMEM((count, SUB, channels), jnp.float32),
            pltpu.SemaphoreType.DMA((count,)),
            pltpu.SemaphoreType.DMA((count,)),
            pltpu.SemaphoreType.DMA((count,)),
            pltpu.SemaphoreType.DMA((count,)),
        ]
        + held
        + landed,
        compiler_params=pltpu.CompilerParams(
            collective_id=1, has_side_effects=True, vmem_limit_bytes=40 * 1024 * 1024
        ),
        cost_estimate=pl.CostEstimate(
            flops=2 * frames * scans * PREC * (channels - PREC),
            bytes_accessed=4 * frames * scans * channels,
            transcendentals=0,
        ),
    )(
        estimate.reshape(frames * scans, channels),
        prec_window.reshape(rows, 1),
        frag_window.reshape(1, columns),
    )


def local(observed, frame_kernel, scan_kernel, prec_window, frag_window):
    estimate = deblur(observed, frame_kernel, scan_kernel)
    return (estimate, correlate(estimate, prec_window, frag_window))


def solution(mesh):
    placed = (P("rt", "mob", None), P(), P(), P("rt"), P("mob"))
    return jax.shard_map(
        local,
        mesh=mesh,
        in_specs=placed,
        out_specs=(P("rt", "mob", None), P("rt", "mob")),
        check_vma=False,
    )
```

```python
import functools

import jax
import jax.numpy as jnp
from jax import lax
from jax.experimental import pallas as pl
from jax.experimental.pallas import tpu as pltpu
from jax.sharding import PartitionSpec as P

PREC = 256
ITERS = 2
LANES = 128
SUB = 8
STEP = 16
AHEAD = 2
CHUNKS = 2


def flipped(k_ref, flip):
    count = k_ref.shape[0]
    return [k_ref[count - 1 - a if flip else a] for a in range(count)]


def blur_scans(taps, src, scans, emit):
    radius = (len(taps) - 1) // 2

    def one(frame, carry):
        total = None
        for a, tap in enumerate(taps):
            part = tap * src[frame, pl.ds(SUB - radius + a, scans), :]
            total = part if total is None else total + part
        emit(frame, total)
        return carry

    lax.fori_loop(0, src.shape[0], one, 0, unroll=4)


def blur_frames(scalars, src, frames, emit):
    count = len(scalars)
    taps = [jnp.full((SUB, LANES), tap, jnp.float32) for tap in scalars]
    rows_of = src.shape[1] // SUB

    def block(index, carry):
        first = (index // rows_of) * STEP
        start = lax.rem(index, rows_of) * SUB
        rows = pl.ds(pl.multiple_of(start, SUB), SUB)
        totals = [None] * STEP
        for j in range(STEP + count - 1):
            value = src[first + j, rows, :]
            for i in range(STEP):
                if 0 <= j - i < count:
                    part = taps[j - i] * value
                    totals[i] = part if totals[i] is None else totals[i] + part
        for i in range(STEP):
            emit(first + i, start, totals[i])
        return carry

    lax.fori_loop(0, (frames // STEP) * rows_of, block, 0)


def deblur_body(sizes, fk_ref, sk_ref, obs_ref, out_ref, *scratch):
    est, blurred, ratio, back, send, recv, swap_send, swap_recv, own_sem = scratch
    rt_size, mob_size = sizes
    frames, scans, channels = obs_ref.shape
    half = channels // 2
    tiles = half // LANES
    long = 2 * frames
    radius = (fk_ref.shape[0] - 1) // 2
    rt, mob = lax.axis_index("rt"), lax.axis_index("mob")
    side = lax.rem(rt, 2)
    mid = pl.ds(SUB, scans)
    has = {
        ("rt", 0): rt >= 2,
        ("rt", 1): rt < rt_size - 2,
        ("mob", 0): mob > 0,
        ("mob", 1): mob < mob_size - 1,
    }
    to = {
        ("rt", 0): lax.rem(rt + rt_size - 2, rt_size),
        ("rt", 1): lax.rem(rt + 2, rt_size),
        ("mob", 0): lax.rem(mob + mob_size - 1, mob_size),
        ("mob", 1): lax.rem(mob + 1, mob_size),
    }
    mate = lax.bitwise_xor(rt, 1)
    mesh_type = pl.DeviceIdType.MESH

    barrier = pltpu.get_barrier_semaphore()
    pl.semaphore_signal(barrier, inc=1, device_id={"rt": mate}, device_id_type=mesh_type)
    for key in has:

        @pl.when(has[key])
        def _(key=key):
            pl.semaphore_signal(
                barrier, inc=1, device_id={key[0]: to[key]}, device_id_type=mesh_type
            )

    peers = 1
    for key in has:
        peers = peers + has[key].astype(jnp.int32)
    pl.semaphore_wait(barrier, peers)

    def lanes_of(which, c):
        return pl.ds(pl.multiple_of(which * half + c * LANES, LANES), LANES)

    def landing(c):
        return est.at[0, c, pl.ds(side * frames, frames), mid, :]

    def swap_in_remote(c):
        return pltpu.make_async_remote_copy(
            src_ref=obs_ref.at[:, :, lanes_of(1 - side, c)],
            dst_ref=landing(c),
            send_sem=swap_send.at[0, c],
            recv_sem=swap_recv.at[0, c],
            device_id={"rt": mate},
            device_id_type=mesh_type,
        )

    def swap_in(c):
        own = pltpu.make_async_copy(
            obs_ref.at[:, :, lanes_of(side, c)], landing(c), own_sem.at[0, c]
        )
        return swap_in_remote(c), own

    def swap_out(c):
        away = pltpu.make_async_remote_copy(
            src_ref=est.at[ITERS, c, pl.ds((1 - side) * frames, frames), mid, :],
            dst_ref=out_ref.at[:, :, lanes_of(side, c)],
            send_sem=swap_send.at[1, c],
            recv_sem=swap_recv.at[1, c],
            device_id={"rt": mate},
            device_id_type=mesh_type,
        )
        own = pltpu.make_async_copy(
            est.at[ITERS, c, pl.ds(side * frames, frames), mid, :],
            out_ref.at[:, :, lanes_of(side, c)],
            own_sem.at[1, c],
        )
        return away, own

    def start_both(pair):
        pair[0].start()
        pair[1].start()

    fields = (est, blurred, ratio, back)

    def halo(kind, it, c, way):
        cells = fields[kind].at[it, c]
        if kind in (0, 3):
            axis = "mob"
            src = cells.at[:, pl.ds(scans if way else SUB, SUB), :]
            dst = cells.at[:, pl.ds(0 if way else SUB + scans, SUB), :]
        else:
            axis = "rt"
            src = cells.at[pl.ds(long if way else radius, radius)]
            dst = cells.at[pl.ds(0 if way else radius + long, radius)]
        return axis, pltpu.make_async_remote_copy(
            src_ref=src,
            dst_ref=dst,
            send_sem=send.at[kind, it, c, way],
            recv_sem=recv.at[kind, it, c, way],
            device_id={axis: to[axis, way]},
            device_id_type=mesh_type,
        )

    def on_halo(kind, it, c, act, flip):
        axis = "mob" if kind in (0, 3) else "rt"
        for way in (0, 1):

            @pl.when(has[axis, 1 - way if flip else way])
            def _(way=way):
                act(halo(kind, it, c, way)[1])

    def start_halo(kind, it, c):
        on_halo(kind, it, c, lambda copy: copy.start(), False)

    def wait_halo(kind, it, c):
        on_halo(kind, it, c, lambda copy: copy.wait_recv(), True)

    def begin(c, carry):
        start_both(swap_in(c))
        return carry

    lax.fori_loop(0, min(AHEAD, tiles), begin, 0)

    def clear(index, carry):
        it, c = index // tiles, lax.rem(index, tiles)
        for field in (est, back):
            for way, start in ((0, 0), (1, SUB + scans)):

                @pl.when(jnp.logical_not(has["mob", way]))
                def _(field=field, start=start):
                    field[it, c, :, pl.ds(start, SUB), :] = jnp.zeros(
                        (long, SUB, LANES), jnp.float32
                    )

        for field in (blurred, ratio):
            for way, start in ((0, 0), (1, radius + long)):

                @pl.when(jnp.logical_not(has["rt", way]))
                def _(field=field, start=start):
                    field[it, c, pl.ds(start, radius)] = jnp.zeros(
                        (radius, scans, LANES), jnp.float32
                    )

        return carry

    lax.fori_loop(0, ITERS * tiles, clear, 0)

    def arrive(c):
        away, own = swap_in(c)
        own.wait()
        away.wait_recv()

        @pl.when(c + AHEAD < tiles)
        def _():
            start_both(swap_in(c + AHEAD))

        start_halo(0, 0, c)

    def forward_scans(it, c):
        wait_halo(0, it, c)

        def emit(frame, total):
            blurred[it, c, radius + frame] = total

        blur_scans(flipped(sk_ref, False), est.at[it, c], scans, emit)
        start_halo(1, it, c)

    def forward_frames(it, c):
        wait_halo(1, it, c)

        def emit(frame, start, total):
            seen = est[0, c, frame, pl.ds(pl.multiple_of(SUB + start, SUB), SUB), :]
            ratio[it, c, radius + frame, pl.ds(pl.multiple_of(start, SUB), SUB), :] = seen / total

        blur_frames(flipped(fk_ref, False), blurred.at[it, c], long, emit)
        start_halo(2, it, c)

    def back_frames(it, c):
        wait_halo(2, it, c)

        def emit(frame, start, total):
            back[it, c, frame, pl.ds(pl.multiple_of(SUB + start, SUB), SUB), :] = total

        blur_frames(flipped(fk_ref, True), ratio.at[it, c], long, emit)
        start_halo(3, it, c)

    def back_scans(it, c):
        wait_halo(3, it, c)

        def emit(frame, total):
            est[it + 1, c, frame, mid, :] = est[it, c, frame, mid, :] * total

        blur_scans(flipped(sk_ref, True), back.at[it, c], scans, emit)

        @pl.when(it < ITERS - 1)
        def _():
            start_halo(0, it + 1, c)

        @pl.when(it == ITERS - 1)
        def _():
            start_both(swap_out(c))

    steps = (forward_scans, forward_frames, back_frames, back_scans)
    total_steps = len(steps) * ITERS
    arrive(0)

    def wave(t, carry):
        def tile(c, inner):
            stage = t - c
            live = jnp.logical_and(stage >= 0, stage < total_steps)
            for n, step in enumerate(steps):

                @pl.when(jnp.logical_and(live, lax.rem(stage + total_steps, len(steps)) == n))
                def _(step=step):
                    step(stage // len(steps), c)

            return inner

        lax.fori_loop(0, tiles, tile, 0)

        @pl.when(t + 1 < tiles)
        def _():
            arrive(t + 1)

        return carry

    lax.fori_loop(0, total_steps + tiles - 1, wave, 0)

    def finish(c, carry):
        away, own = swap_out(c)
        own.wait()
        away.wait()
        swap_in_remote(c).wait_send()
        return carry

    lax.fori_loop(0, tiles, finish, 0)

    def sent(index, carry):
        it, c = index // tiles, lax.rem(index, tiles)
        for kind in range(len(fields)):
            on_halo(kind, it, c, lambda copy: copy.wait_send(), False)
        return carry

    lax.fori_loop(0, ITERS * tiles, sent, 0)


def deblur(observed, frame_kernel, scan_kernel):
    frames, scans, channels = observed.shape
    tiles = channels // 2 // LANES
    radius = (frame_kernel.shape[0] - 1) // 2
    sizes = lax.axis_size("rt"), lax.axis_size("mob")
    tall = (2 * frames, scans + 2 * SUB, LANES)
    long = (2 * frames + 2 * radius, scans, LANES)
    smem = pl.BlockSpec(memory_space=pltpu.SMEM)
    anywhere = pl.BlockSpec(memory_space=pl.ANY)
    dma = pltpu.SemaphoreType.DMA
    return pl.pallas_call(
        functools.partial(deblur_body, sizes),
        in_specs=[smem, smem, anywhere],
        out_specs=anywhere,
        out_shape=jax.ShapeDtypeStruct(observed.shape, jnp.float32),
        scratch_shapes=[
            pltpu.VMEM((ITERS + 1, tiles) + tall, jnp.float32),
            pltpu.VMEM((ITERS, tiles) + long, jnp.float32),
            pltpu.VMEM((ITERS, tiles) + long, jnp.float32),
            pltpu.VMEM((ITERS, tiles) + tall, jnp.float32),
            dma((4, ITERS, tiles, 2)),
            dma((4, ITERS, tiles, 2)),
            dma((2, tiles)),
            dma((2, tiles)),
            dma((2, tiles)),
        ],
        compiler_params=pltpu.CompilerParams(
            collective_id=2, has_side_effects=True, vmem_limit_bytes=50 * 1024 * 1024
        ),
        cost_estimate=pl.CostEstimate(
            flops=4 * ITERS * (frame_kernel.shape[0] + scan_kernel.shape[0]) * observed.size,
            bytes_accessed=8 * observed.size,
            transcendentals=0,
        ),
    )(frame_kernel, scan_kernel, observed)


def partner(axis, bit):
    return lax.bitwise_xor(lax.axis_index(axis), bit)


def bits_of(size):
    return [1 << n for n in range(size.bit_length() - 1)]


def greet(stages):
    barrier = pltpu.get_barrier_semaphore()
    for axis, bit in stages:
        pl.semaphore_signal(
            barrier,
            inc=1,
            device_id={axis: partner(axis, bit)},
            device_id_type=pl.DeviceIdType.MESH,
        )
    pl.semaphore_wait(barrier, len(stages))


def exchange(src, dst, send_sem, recv_sem, stage):
    axis, bit = stage
    copy = pltpu.make_async_remote_copy(
        src_ref=src,
        dst_ref=dst,
        send_sem=send_sem,
        recv_sem=recv_sem,
        device_id={axis: partner(axis, bit)},
        device_id_type=pl.DeviceIdType.MESH,
    )
    copy.start()
    return copy


def correlate_body(stages, groups, cells, est_ref, prow_ref, fcol_ref, out_ref, *scratch):
    count = len(stages)
    sums, got, sum_send, sum_recv, send_sem, recv_sem = scratch[:6]
    held = scratch[6 : 6 + count]
    landed = scratch[6 + count :]
    mobs, rows_of = groups
    prec = est_ref.shape[1] - mobs * out_ref.shape[1]
    rows, columns = out_ref.shape
    part = columns // CHUNKS
    greet(stages)
    here = jnp.sum(est_ref[...], axis=0, keepdims=True)
    lane_tiles = est_ref.shape[1] // LANES
    sums[0] = jnp.zeros(sums.shape[1:], jnp.float32)
    for k in range(lane_tiles):
        sums[0, k : k + 1, :] = here[:, k * LANES : (k + 1) * LANES]
    for n, stage in enumerate(stages):
        copy = exchange(sums.at[n], got.at[n], sum_send.at[n], sum_recv.at[n], stage)
        copy.wait()
        sums[n + 1] = sums[n] + got[n]
    mean = jnp.concatenate([sums[count, k : k + 1, :] for k in range(lane_tiles)], axis=1) / cells
    left = (est_ref[:, :prec] - mean[:, :prec]).astype(jnp.bfloat16)
    wide = left.astype(jnp.float32)
    left_squares = jnp.sum(wide * wide, axis=0, keepdims=True)
    across = left.T
    first = held[0]
    upper = lax.broadcasted_iota(jnp.int32, (SUB, columns), 0) < SUB // 2
    for m in range(mobs):
        start = prec + m * columns
        right = (
            est_ref[:, start : start + columns] - mean[:, start : start + columns]
        ).astype(jnp.bfloat16)
        wide = right.astype(jnp.float32)
        right_squares = jnp.sum(wide * wide, axis=0, keepdims=True)
        squares = jnp.where(upper, right_squares, left_squares)
        product = jnp.dot(across, right, preferred_element_type=jnp.float32)
        for r in range(rows_of):
            for k in range(CHUNKS):
                block = first.at[k, m // 2, m % 2, r]
                block[:rows, :] = product[r * rows : (r + 1) * rows, k * part : (k + 1) * part]
                block[rows:, :] = squares[:, k * part : (k + 1) * part]

    def send_chunk(n, k):
        axis, bit = stages[n]
        mine = lax.rem(lax.axis_index(axis) // bit, 2)
        return exchange(
            held[n].at[k, :, 1 - mine],
            landed[n].at[k],
            send_sem.at[n, k],
            recv_sem.at[n, k],
            stages[n],
        )

    copies = [send_chunk(0, k) for k in range(CHUNKS)]
    totals = [None] * CHUNKS
    for n, (axis, bit) in enumerate(stages):
        mine = lax.rem(lax.axis_index(axis) // bit, 2)
        for k in range(CHUNKS):
            copies[k].wait()
            for i in range(held[n].shape[1]):
                total = held[n][k, i, mine] + landed[n][k, i]
                if n + 1 == count:
                    totals[k] = total
                elif stages[n + 1][0] == axis:
                    held[n + 1][k, i // 2, i % 2] = total
                else:
                    for r in range(rows_of):
                        held[n + 1][k, r // 2, r % 2] = total[r]
            if n + 1 < count:
                copies[k] = send_chunk(n + 1, k)
    total = jnp.concatenate(totals, axis=1)
    column = 1.0 / jnp.sqrt(total[rows : rows + 1, :] + 1e-06)
    row = 1.0 / jnp.sqrt(total[rows + SUB // 2 : rows + SUB // 2 + 1, :] + 1e-06)
    place = lax.broadcasted_iota(jnp.int32, (rows, prec), 1)
    wanted = lax.broadcasted_iota(jnp.int32, (rows, prec), 0) + lax.axis_index("rt") * rows
    row = jnp.sum(jnp.where(place == wanted, row, 0.0), axis=1, keepdims=True)
    same = (prow_ref[...] == fcol_ref[...]).astype(jnp.float32)
    out_ref[...] = same * total[:rows, :] * row * column


def correlate(estimate, prec_window, frag_window):
    frames, scans, channels = estimate.shape
    mobs, rows_of = lax.axis_size("mob"), lax.axis_size("rt")
    rows, columns = prec_window.shape[0], frag_window.shape[0]
    stages = [("mob", bit) for bit in bits_of(mobs)] + [("rt", bit) for bit in bits_of(rows_of)]
    count = len(stages)
    tile = (rows + SUB, columns // CHUNKS)
    sum_rows = -(-channels // (LANES * SUB)) * SUB
    held, landed = [], []
    for axis, bit in stages:
        if axis == "mob":
            span, tail = mobs // (2 * bit), (rows_of,) + tile
        else:
            span, tail = rows_of // (2 * bit), tile
        held.append(pltpu.VMEM((CHUNKS, span, 2) + tail, jnp.float32))
        landed.append(pltpu.VMEM((CHUNKS, span) + tail, jnp.float32))
    whole = pl.BlockSpec(memory_space=pltpu.VMEM)
    cells = frames * scans * mobs * rows_of
    return pl.pallas_call(
        functools.partial(correlate_body, stages, (mobs, rows_of), cells),
        in_specs=[whole] * 3,
        out_specs=whole,
        out_shape=jax.ShapeDtypeStruct((rows, columns), jnp.float32),
        scratch_shapes=[
            pltpu.VMEM((count + 1, sum_rows, LANES), jnp.float32),
            pltpu.VMEM((count, sum_rows, LANES), jnp.float32),
            pltpu.SemaphoreType.DMA((count,)),
            pltpu.SemaphoreType.DMA((count,)),
            pltpu.SemaphoreType.DMA((count, CHUNKS)),
            pltpu.SemaphoreType.DMA((count, CHUNKS)),
        ]
        + held
        + landed,
        compiler_params=pltpu.CompilerParams(
            collective_id=1, has_side_effects=True, vmem_limit_bytes=40 * 1024 * 1024
        ),
        cost_estimate=pl.CostEstimate(
            flops=2 * frames * scans * PREC * (channels - PREC),
            bytes_accessed=4 * frames * scans * channels,
            transcendentals=0,
        ),
    )(
        estimate.reshape(frames * scans, channels),
        prec_window.reshape(rows, 1),
        frag_window.reshape(1, columns),
    )


def local(observed, frame_kernel, scan_kernel, prec_window, frag_window):
    estimate = deblur(observed, frame_kernel, scan_kernel)
    return (estimate, correlate(estimate, prec_window, frag_window))


def solution(mesh):
    placed = (P("rt", "mob", None), P(), P(), P("rt"), P("mob"))
    return jax.shard_map(
        local,
        mesh=mesh,
        in_specs=placed,
        out_specs=(P("rt", "mob", None), P("rt", "mob")),
        check_vma=False,
    )
```

```python
import functools

import jax
import jax.numpy as jnp
from jax import lax
from jax.experimental import pallas as pl
from jax.experimental.pallas import tpu as pltpu
from jax.sharding import PartitionSpec as P

PREC = 256
ITERS = 2
LANES = 128
SUB = 8
STEP = 16
AHEAD = 2
CHUNKS = 2


def flipped(k_ref, flip):
    count = k_ref.shape[0]
    return [k_ref[count - 1 - a if flip else a] for a in range(count)]


def blur_scans(taps, src, scans, emit):
    radius = (len(taps) - 1) // 2

    def one(frame, carry):
        total = None
        for a, tap in enumerate(taps):
            part = tap * src[frame, pl.ds(SUB - radius + a, scans), :]
            total = part if total is None else total + part
        emit(frame, total)
        return carry

    lax.fori_loop(0, src.shape[0], one, 0, unroll=4)


def blur_frames(scalars, src, frames, emit):
    count = len(scalars)
    taps = [jnp.full((SUB, LANES), tap, jnp.float32) for tap in scalars]
    rows_of = src.shape[1] // SUB

    def block(index, carry):
        first = (index // rows_of) * STEP
        start = lax.rem(index, rows_of) * SUB
        rows = pl.ds(pl.multiple_of(start, SUB), SUB)
        totals = [None] * STEP
        for j in range(STEP + count - 1):
            value = src[first + j, rows, :]
            for i in range(STEP):
                if 0 <= j - i < count:
                    part = taps[j - i] * value
                    totals[i] = part if totals[i] is None else totals[i] + part
        for i in range(STEP):
            emit(first + i, start, totals[i])
        return carry

    lax.fori_loop(0, (frames // STEP) * rows_of, block, 0)


def deblur_body(sizes, fk_ref, sk_ref, obs_ref, out_ref, *scratch):
    est, blurred, ratio, back, send, recv, swap_send, swap_recv, own_sem = scratch
    rt_size, mob_size = sizes
    frames, scans, channels = obs_ref.shape
    half = channels // 2
    tiles = half // LANES
    long = 2 * frames
    radius = (fk_ref.shape[0] - 1) // 2
    rt, mob = lax.axis_index("rt"), lax.axis_index("mob")
    side = lax.rem(rt, 2)
    mid = pl.ds(SUB, scans)
    has = {
        ("rt", 0): rt >= 2,
        ("rt", 1): rt < rt_size - 2,
        ("mob", 0): mob > 0,
        ("mob", 1): mob < mob_size - 1,
    }
    to = {
        ("rt", 0): lax.rem(rt + rt_size - 2, rt_size),
        ("rt", 1): lax.rem(rt + 2, rt_size),
        ("mob", 0): lax.rem(mob + mob_size - 1, mob_size),
        ("mob", 1): lax.rem(mob + 1, mob_size),
    }
    mate = lax.bitwise_xor(rt, 1)
    mesh_type = pl.DeviceIdType.MESH

    barrier = pltpu.get_barrier_semaphore()
    pl.semaphore_signal(barrier, inc=1, device_id={"rt": mate}, device_id_type=mesh_type)
    for key in has:

        @pl.when(has[key])
        def _(key=key):
            pl.semaphore_signal(
                barrier, inc=1, device_id={key[0]: to[key]}, device_id_type=mesh_type
            )

    peers = 1
    for key in has:
        peers = peers + has[key].astype(jnp.int32)
    pl.semaphore_wait(barrier, peers)

    def lanes_of(which, c):
        return pl.ds(pl.multiple_of(which * half + c * LANES, LANES), LANES)

    def landing(c):
        return est.at[0, c, pl.ds(side * frames, frames), mid, :]

    def swap_in_remote(c):
        return pltpu.make_async_remote_copy(
            src_ref=obs_ref.at[:, :, lanes_of(1 - side, c)],
            dst_ref=landing(c),
            send_sem=swap_send.at[0, c],
            recv_sem=swap_recv.at[0, c],
            device_id={"rt": mate},
            device_id_type=mesh_type,
        )

    def swap_in(c):
        own = pltpu.make_async_copy(
            obs_ref.at[:, :, lanes_of(side, c)], landing(c), own_sem.at[0, c]
        )
        return swap_in_remote(c), own

    def swap_out(c):
        away = pltpu.make_async_remote_copy(
            src_ref=est.at[ITERS, c, pl.ds((1 - side) * frames, frames), mid, :],
            dst_ref=out_ref.at[:, :, lanes_of(side, c)],
            send_sem=swap_send.at[1, c],
            recv_sem=swap_recv.at[1, c],
            device_id={"rt": mate},
            device_id_type=mesh_type,
        )
        own = pltpu.make_async_copy(
            est.at[ITERS, c, pl.ds(side * frames, frames), mid, :],
            out_ref.at[:, :, lanes_of(side, c)],
            own_sem.at[1, c],
        )
        return away, own

    def start_both(pair):
        pair[0].start()
        pair[1].start()

    fields = (est, blurred, ratio, back)

    def halo(kind, it, c, way):
        cells = fields[kind].at[it, c]
        if kind in (0, 3):
            axis = "mob"
            src = cells.at[:, pl.ds(scans if way else SUB, SUB), :]
            dst = cells.at[:, pl.ds(0 if way else SUB + scans, SUB), :]
        else:
            axis = "rt"
            src = cells.at[pl.ds(long if way else radius, radius)]
            dst = cells.at[pl.ds(0 if way else radius + long, radius)]
        return axis, pltpu.make_async_remote_copy(
            src_ref=src,
            dst_ref=dst,
            send_sem=send.at[kind, it, c, way],
            recv_sem=recv.at[kind, it, c, way],
            device_id={axis: to[axis, way]},
            device_id_type=mesh_type,
        )

    def on_halo(kind, it, c, act, flip):
        axis = "mob" if kind in (0, 3) else "rt"
        for way in (0, 1):

            @pl.when(has[axis, 1 - way if flip else way])
            def _(way=way):
                act(halo(kind, it, c, way)[1])

    def start_halo(kind, it, c):
        on_halo(kind, it, c, lambda copy: copy.start(), False)

    def wait_halo(kind, it, c):
        on_halo(kind, it, c, lambda copy: copy.wait_recv(), True)

    def begin(c, carry):
        start_both(swap_in(c))
        return carry

    lax.fori_loop(0, min(AHEAD, tiles), begin, 0)

    def clear(index, carry):
        it, c = index // tiles, lax.rem(index, tiles)
        for field in (est, back):
            for way, start in ((0, 0), (1, SUB + scans)):

                @pl.when(jnp.logical_not(has["mob", way]))
                def _(field=field, start=start):
                    field[it, c, :, pl.ds(start, SUB), :] = jnp.zeros(
                        (long, SUB, LANES), jnp.float32
                    )

        for field in (blurred, ratio):
            for way, start in ((0, 0), (1, radius + long)):

                @pl.when(jnp.logical_not(has["rt", way]))
                def _(field=field, start=start):
                    field[it, c, pl.ds(start, radius)] = jnp.zeros(
                        (radius, scans, LANES), jnp.float32
                    )

        return carry

    lax.fori_loop(0, ITERS * tiles, clear, 0)

    def arrive(c):
        away, own = swap_in(c)
        own.wait()
        away.wait_recv()

        @pl.when(c + AHEAD < tiles)
        def _():
            start_both(swap_in(c + AHEAD))

        start_halo(0, 0, c)

    def forward_scans(it, c):
        wait_halo(0, it, c)

        def emit(frame, total):
            blurred[it, c, radius + frame] = total

        blur_scans(flipped(sk_ref, False), est.at[it, c], scans, emit)
        start_halo(1, it, c)

    def forward_frames(it, c):
        wait_halo(1, it, c)

        def emit(frame, start, total):
            seen = est[0, c, frame, pl.ds(pl.multiple_of(SUB + start, SUB), SUB), :]
            ratio[it, c, radius + frame, pl.ds(pl.multiple_of(start, SUB), SUB), :] = seen / total

        blur_frames(flipped(fk_ref, False), blurred.at[it, c], long, emit)
        start_halo(2, it, c)

    def back_frames(it, c):
        wait_halo(2, it, c)

        def emit(frame, start, total):
            back[it, c, frame, pl.ds(pl.multiple_of(SUB + start, SUB), SUB), :] = total

        blur_frames(flipped(fk_ref, True), ratio.at[it, c], long, emit)
        start_halo(3, it, c)

    def back_scans(it, c):
        wait_halo(3, it, c)

        def emit(frame, total):
            est[it + 1, c, frame, mid, :] = est[it, c, frame, mid, :] * total

        blur_scans(flipped(sk_ref, True), back.at[it, c], scans, emit)

        @pl.when(it < ITERS - 1)
        def _():
            start_halo(0, it + 1, c)

        @pl.when(it == ITERS - 1)
        def _():
            start_both(swap_out(c))

    steps = (forward_scans, forward_frames, back_frames, back_scans)
    total_steps = len(steps) * ITERS
    arrive(0)

    def wave(t, carry):
        def tile(c, inner):
            stage = t - c
            live = jnp.logical_and(stage >= 0, stage < total_steps)
            for n, step in enumerate(steps):

                @pl.when(jnp.logical_and(live, lax.rem(stage + total_steps, len(steps)) == n))
                def _(step=step):
                    step(stage // len(steps), c)

            return inner

        lax.fori_loop(0, tiles, tile, 0)

        @pl.when(t + 1 < tiles)
        def _():
            arrive(t + 1)

        return carry

    lax.fori_loop(0, total_steps + tiles - 1, wave, 0)

    def finish(c, carry):
        away, own = swap_out(c)
        own.wait()
        away.wait()
        swap_in_remote(c).wait_send()
        return carry

    lax.fori_loop(0, tiles, finish, 0)

    def sent(index, carry):
        it, c = index // tiles, lax.rem(index, tiles)
        for kind in range(len(fields)):
            on_halo(kind, it, c, lambda copy: copy.wait_send(), False)
        return carry

    lax.fori_loop(0, ITERS * tiles, sent, 0)


def deblur(observed, frame_kernel, scan_kernel):
    frames, scans, channels = observed.shape
    tiles = channels // 2 // LANES
    radius = (frame_kernel.shape[0] - 1) // 2
    sizes = lax.axis_size("rt"), lax.axis_size("mob")
    tall = (2 * frames, scans + 2 * SUB, LANES)
    long = (2 * frames + 2 * radius, scans, LANES)
    smem = pl.BlockSpec(memory_space=pltpu.SMEM)
    anywhere = pl.BlockSpec(memory_space=pl.ANY)
    dma = pltpu.SemaphoreType.DMA
    return pl.pallas_call(
        functools.partial(deblur_body, sizes),
        in_specs=[smem, smem, anywhere],
        out_specs=anywhere,
        out_shape=jax.ShapeDtypeStruct(observed.shape, jnp.float32),
        scratch_shapes=[
            pltpu.VMEM((ITERS + 1, tiles) + tall, jnp.float32),
            pltpu.VMEM((ITERS, tiles) + long, jnp.float32),
            pltpu.VMEM((ITERS, tiles) + long, jnp.float32),
            pltpu.VMEM((ITERS, tiles) + tall, jnp.float32),
            dma((4, ITERS, tiles, 2)),
            dma((4, ITERS, tiles, 2)),
            dma((2, tiles)),
            dma((2, tiles)),
            dma((2, tiles)),
        ],
        compiler_params=pltpu.CompilerParams(
            collective_id=2, has_side_effects=True, vmem_limit_bytes=50 * 1024 * 1024
        ),
        cost_estimate=pl.CostEstimate(
            flops=4 * ITERS * (frame_kernel.shape[0] + scan_kernel.shape[0]) * observed.size,
            bytes_accessed=8 * observed.size,
            transcendentals=0,
        ),
    )(frame_kernel, scan_kernel, observed)


def partner(axis, bit):
    return lax.bitwise_xor(lax.axis_index(axis), bit)


def bits_of(size):
    return [1 << n for n in range(size.bit_length() - 1)]


def greet(stages):
    barrier = pltpu.get_barrier_semaphore()
    for axis, bit in stages:
        pl.semaphore_signal(
            barrier,
            inc=1,
            device_id={axis: partner(axis, bit)},
            device_id_type=pl.DeviceIdType.MESH,
        )
    pl.semaphore_wait(barrier, len(stages))


def exchange(src, dst, send_sem, recv_sem, stage):
    axis, bit = stage
    copy = pltpu.make_async_remote_copy(
        src_ref=src,
        dst_ref=dst,
        send_sem=send_sem,
        recv_sem=recv_sem,
        device_id={axis: partner(axis, bit)},
        device_id_type=pl.DeviceIdType.MESH,
    )
    copy.start()
    return copy


def correlate_body(stages, groups, cells, est_ref, prow_ref, fcol_ref, out_ref, *scratch):
    count = len(stages)
    sums, got, sum_send, sum_recv, send_sem, recv_sem = scratch[:6]
    held = scratch[6 : 6 + count]
    landed = scratch[6 + count :]
    mobs, rows_of = groups
    prec = est_ref.shape[1] - mobs * out_ref.shape[1]
    rows, columns = out_ref.shape
    part = columns // CHUNKS
    peers = [("mob", n) for n in range(1, mobs)] + [("rt", n) for n in range(1, rows_of)]
    greet(peers)
    here = jnp.sum(est_ref[...], axis=0, keepdims=True)
    lane_tiles = est_ref.shape[1] // LANES
    sums[0] = jnp.zeros(sums.shape[1:], jnp.float32)
    for k in range(lane_tiles):
        sums[0, k : k + 1, :] = here[:, k * LANES : (k + 1) * LANES]
    for n, axis in enumerate(("mob", "rt")):
        slots = [i for i, peer in enumerate(peers) if peer[0] == axis]
        flying = [
            exchange(sums.at[n], got.at[i], sum_send.at[i], sum_recv.at[i], peers[i])
            for i in slots
        ]
        total = sums[n]
        for i, copy in zip(slots, flying):
            copy.wait()
            total = total + got[i]
        sums[n + 1] = total
    mean = jnp.concatenate([sums[2, k : k + 1, :] for k in range(lane_tiles)], axis=1) / cells
    left = (est_ref[:, :prec] - mean[:, :prec]).astype(jnp.bfloat16)
    wide = left.astype(jnp.float32)
    left_squares = jnp.sum(wide * wide, axis=0, keepdims=True)
    across = left.T
    first = held[0]
    upper = lax.broadcasted_iota(jnp.int32, (SUB, columns), 0) < SUB // 2
    for m in range(mobs):
        start = prec + m * columns
        right = (
            est_ref[:, start : start + columns] - mean[:, start : start + columns]
        ).astype(jnp.bfloat16)
        wide = right.astype(jnp.float32)
        right_squares = jnp.sum(wide * wide, axis=0, keepdims=True)
        squares = jnp.where(upper, right_squares, left_squares)
        product = jnp.dot(across, right, preferred_element_type=jnp.float32)
        for r in range(rows_of):
            for k in range(CHUNKS):
                block = first.at[k, m // 2, m % 2, r]
                block[:rows, :] = product[r * rows : (r + 1) * rows, k * part : (k + 1) * part]
                block[rows:, :] = squares[:, k * part : (k + 1) * part]

    def send_chunk(n, k):
        axis, bit = stages[n]
        mine = lax.rem(lax.axis_index(axis) // bit, 2)
        return exchange(
            held[n].at[k, :, 1 - mine],
            landed[n].at[k],
            send_sem.at[n, k],
            recv_sem.at[n, k],
            stages[n],
        )

    copies = [send_chunk(0, k) for k in range(CHUNKS)]
    totals = [None] * CHUNKS
    for n, (axis, bit) in enumerate(stages):
        mine = lax.rem(lax.axis_index(axis) // bit, 2)
        for k in range(CHUNKS):
            copies[k].wait()
            for i in range(held[n].shape[1]):
                total = held[n][k, i, mine] + landed[n][k, i]
                if n + 1 == count:
                    totals[k] = total
                elif stages[n + 1][0] == axis:
                    held[n + 1][k, i // 2, i % 2] = total
                else:
                    for r in range(rows_of):
                        held[n + 1][k, r // 2, r % 2] = total[r]
            if n + 1 < count:
                copies[k] = send_chunk(n + 1, k)
    total = jnp.concatenate(totals, axis=1)
    column = 1.0 / jnp.sqrt(total[rows : rows + 1, :] + 1e-06)
    row = 1.0 / jnp.sqrt(total[rows + SUB // 2 : rows + SUB // 2 + 1, :] + 1e-06)
    place = lax.broadcasted_iota(jnp.int32, (rows, prec), 1)
    wanted = lax.broadcasted_iota(jnp.int32, (rows, prec), 0) + lax.axis_index("rt") * rows
    row = jnp.sum(jnp.where(place == wanted, row, 0.0), axis=1, keepdims=True)
    same = (prow_ref[...] == fcol_ref[...]).astype(jnp.float32)
    out_ref[...] = same * total[:rows, :] * row * column


def correlate(estimate, prec_window, frag_window):
    frames, scans, channels = estimate.shape
    mobs, rows_of = lax.axis_size("mob"), lax.axis_size("rt")
    rows, columns = prec_window.shape[0], frag_window.shape[0]
    stages = [("mob", bit) for bit in bits_of(mobs)] + [("rt", bit) for bit in bits_of(rows_of)]
    count = len(stages)
    peers = mobs + rows_of - 2
    tile = (rows + SUB, columns // CHUNKS)
    sum_rows = -(-channels // (LANES * SUB)) * SUB
    held, landed = [], []
    for axis, bit in stages:
        if axis == "mob":
            span, tail = mobs // (2 * bit), (rows_of,) + tile
        else:
            span, tail = rows_of // (2 * bit), tile
        held.append(pltpu.VMEM((CHUNKS, span, 2) + tail, jnp.float32))
        landed.append(pltpu.VMEM((CHUNKS, span) + tail, jnp.float32))
    whole = pl.BlockSpec(memory_space=pltpu.VMEM)
    cells = frames * scans * mobs * rows_of
    return pl.pallas_call(
        functools.partial(correlate_body, stages, (mobs, rows_of), cells),
        in_specs=[whole] * 3,
        out_specs=whole,
        out_shape=jax.ShapeDtypeStruct((rows, columns), jnp.float32),
        scratch_shapes=[
            pltpu.VMEM((3, sum_rows, LANES), jnp.float32),
            pltpu.VMEM((peers, sum_rows, LANES), jnp.float32),
            pltpu.SemaphoreType.DMA((peers,)),
            pltpu.SemaphoreType.DMA((peers,)),
            pltpu.SemaphoreType.DMA((count, CHUNKS)),
            pltpu.SemaphoreType.DMA((count, CHUNKS)),
        ]
        + held
        + landed,
        compiler_params=pltpu.CompilerParams(
            collective_id=1, has_side_effects=True, vmem_limit_bytes=40 * 1024 * 1024
        ),
        cost_estimate=pl.CostEstimate(
            flops=2 * frames * scans * PREC * (channels - PREC),
            bytes_accessed=4 * frames * scans * channels,
            transcendentals=0,
        ),
    )(
        estimate.reshape(frames * scans, channels),
        prec_window.reshape(rows, 1),
        frag_window.reshape(1, columns),
    )


def local(observed, frame_kernel, scan_kernel, prec_window, frag_window):
    estimate = deblur(observed, frame_kernel, scan_kernel)
    return (estimate, correlate(estimate, prec_window, frag_window))


def solution(mesh):
    placed = (P("rt", "mob", None), P(), P(), P("rt"), P("mob"))
    return jax.shard_map(
        local,
        mesh=mesh,
        in_specs=placed,
        out_specs=(P("rt", "mob", None), P("rt", "mob")),
        check_vma=False,
    )
```

```python
import functools

import jax
import jax.numpy as jnp
from jax import lax
from jax.experimental import pallas as pl
from jax.experimental.pallas import tpu as pltpu
from jax.sharding import PartitionSpec as P

PREC = 256
ITERS = 2
LANES = 128
SUB = 8
STEP = 16
AHEAD = 2
CHUNKS = 2


def flipped(k_ref, flip):
    count = k_ref.shape[0]
    return [k_ref[count - 1 - a if flip else a] for a in range(count)]


def blur_scans(taps, src, scans, emit):
    radius = (len(taps) - 1) // 2

    def one(frame, carry):
        total = None
        for a, tap in enumerate(taps):
            part = tap * src[frame, pl.ds(SUB - radius + a, scans), :]
            total = part if total is None else total + part
        emit(frame, total)
        return carry

    lax.fori_loop(0, src.shape[0], one, 0, unroll=8)


def blur_frames(scalars, src, frames, emit):
    count = len(scalars)
    taps = [jnp.full((SUB, LANES), tap, jnp.float32) for tap in scalars]
    rows_of = src.shape[1] // SUB

    def block(index, carry):
        first = (index // rows_of) * STEP
        start = lax.rem(index, rows_of) * SUB
        rows = pl.ds(pl.multiple_of(start, SUB), SUB)
        totals = [None] * STEP
        for j in range(STEP + count - 1):
            value = src[first + j, rows, :]
            for i in range(STEP):
                if 0 <= j - i < count:
                    part = taps[j - i] * value
                    totals[i] = part if totals[i] is None else totals[i] + part
        for i in range(STEP):
            emit(first + i, start, totals[i])
        return carry

    lax.fori_loop(0, (frames // STEP) * rows_of, block, 0)


def deblur_body(sizes, fk_ref, sk_ref, obs_ref, out_ref, *scratch):
    est, blurred, ratio, back, send, recv, swap_send, swap_recv, own_sem = scratch
    rt_size, mob_size = sizes
    frames, scans, channels = obs_ref.shape
    half = channels // 2
    tiles = half // LANES
    long = 2 * frames
    radius = (fk_ref.shape[0] - 1) // 2
    rt, mob = lax.axis_index("rt"), lax.axis_index("mob")
    side = lax.rem(rt, 2)
    mid = pl.ds(SUB, scans)
    has = {
        ("rt", 0): rt >= 2,
        ("rt", 1): rt < rt_size - 2,
        ("mob", 0): mob > 0,
        ("mob", 1): mob < mob_size - 1,
    }
    to = {
        ("rt", 0): lax.rem(rt + rt_size - 2, rt_size),
        ("rt", 1): lax.rem(rt + 2, rt_size),
        ("mob", 0): lax.rem(mob + mob_size - 1, mob_size),
        ("mob", 1): lax.rem(mob + 1, mob_size),
    }
    mate = lax.bitwise_xor(rt, 1)
    mesh_type = pl.DeviceIdType.MESH

    barrier = pltpu.get_barrier_semaphore()
    pl.semaphore_signal(barrier, inc=1, device_id={"rt": mate}, device_id_type=mesh_type)
    for key in has:

        @pl.when(has[key])
        def _(key=key):
            pl.semaphore_signal(
                barrier, inc=1, device_id={key[0]: to[key]}, device_id_type=mesh_type
            )

    peers = 1
    for key in has:
        peers = peers + has[key].astype(jnp.int32)
    pl.semaphore_wait(barrier, peers)

    def lanes_of(which, c):
        return pl.ds(pl.multiple_of(which * half + c * LANES, LANES), LANES)

    def landing(c):
        return est.at[0, c, pl.ds(side * frames, frames), mid, :]

    def swap_in_remote(c):
        return pltpu.make_async_remote_copy(
            src_ref=obs_ref.at[:, :, lanes_of(1 - side, c)],
            dst_ref=landing(c),
            send_sem=swap_send.at[0, c],
            recv_sem=swap_recv.at[0, c],
            device_id={"rt": mate},
            device_id_type=mesh_type,
        )

    def swap_in(c):
        own = pltpu.make_async_copy(
            obs_ref.at[:, :, lanes_of(side, c)], landing(c), own_sem.at[0, c]
        )
        return swap_in_remote(c), own

    def swap_out(c):
        away = pltpu.make_async_remote_copy(
            src_ref=est.at[ITERS, c, pl.ds((1 - side) * frames, frames), mid, :],
            dst_ref=out_ref.at[:, :, lanes_of(side, c)],
            send_sem=swap_send.at[1, c],
            recv_sem=swap_recv.at[1, c],
            device_id={"rt": mate},
            device_id_type=mesh_type,
        )
        own = pltpu.make_async_copy(
            est.at[ITERS, c, pl.ds(side * frames, frames), mid, :],
            out_ref.at[:, :, lanes_of(side, c)],
            own_sem.at[1, c],
        )
        return away, own

    def start_both(pair):
        pair[0].start()
        pair[1].start()

    fields = (est, blurred, ratio, back)

    def halo(kind, it, c, way):
        cells = fields[kind].at[it, c]
        if kind in (0, 3):
            axis = "mob"
            src = cells.at[:, pl.ds(scans if way else SUB, SUB), :]
            dst = cells.at[:, pl.ds(0 if way else SUB + scans, SUB), :]
        else:
            axis = "rt"
            src = cells.at[pl.ds(long if way else radius, radius)]
            dst = cells.at[pl.ds(0 if way else radius + long, radius)]
        return axis, pltpu.make_async_remote_copy(
            src_ref=src,
            dst_ref=dst,
            send_sem=send.at[kind, it, c, way],
            recv_sem=recv.at[kind, it, c, way],
            device_id={axis: to[axis, way]},
            device_id_type=mesh_type,
        )

    def on_halo(kind, it, c, act, flip):
        axis = "mob" if kind in (0, 3) else "rt"
        for way in (0, 1):

            @pl.when(has[axis, 1 - way if flip else way])
            def _(way=way):
                act(halo(kind, it, c, way)[1])

    def start_halo(kind, it, c):
        on_halo(kind, it, c, lambda copy: copy.start(), False)

    def wait_halo(kind, it, c):
        on_halo(kind, it, c, lambda copy: copy.wait_recv(), True)

    def begin(c, carry):
        start_both(swap_in(c))
        return carry

    lax.fori_loop(0, min(AHEAD, tiles), begin, 0)

    def clear(index, carry):
        it, c = index // tiles, lax.rem(index, tiles)
        for field in (est, back):
            for way, start in ((0, 0), (1, SUB + scans)):

                @pl.when(jnp.logical_not(has["mob", way]))
                def _(field=field, start=start):
                    field[it, c, :, pl.ds(start, SUB), :] = jnp.zeros(
                        (long, SUB, LANES), jnp.float32
                    )

        for field in (blurred, ratio):
            for way, start in ((0, 0), (1, radius + long)):

                @pl.when(jnp.logical_not(has["rt", way]))
                def _(field=field, start=start):
                    field[it, c, pl.ds(start, radius)] = jnp.zeros(
                        (radius, scans, LANES), jnp.float32
                    )

        return carry

    lax.fori_loop(0, ITERS * tiles, clear, 0)

    def arrive(c):
        away, own = swap_in(c)
        own.wait()
        away.wait_recv()

        @pl.when(c + AHEAD < tiles)
        def _():
            start_both(swap_in(c + AHEAD))

        start_halo(0, 0, c)

    def forward_scans(it, c):
        wait_halo(0, it, c)

        def emit(frame, total):
            blurred[it, c, radius + frame] = total

        blur_scans(flipped(sk_ref, False), est.at[it, c], scans, emit)
        start_halo(1, it, c)

    def forward_frames(it, c):
        wait_halo(1, it, c)

        def emit(frame, start, total):
            seen = est[0, c, frame, pl.ds(pl.multiple_of(SUB + start, SUB), SUB), :]
            ratio[it, c, radius + frame, pl.ds(pl.multiple_of(start, SUB), SUB), :] = seen / total

        blur_frames(flipped(fk_ref, False), blurred.at[it, c], long, emit)
        start_halo(2, it, c)

    def back_frames(it, c):
        wait_halo(2, it, c)

        def emit(frame, start, total):
            back[it, c, frame, pl.ds(pl.multiple_of(SUB + start, SUB), SUB), :] = total

        blur_frames(flipped(fk_ref, True), ratio.at[it, c], long, emit)
        start_halo(3, it, c)

    def back_scans(it, c):
        wait_halo(3, it, c)

        def emit(frame, total):
            est[it + 1, c, frame, mid, :] = est[it, c, frame, mid, :] * total

        blur_scans(flipped(sk_ref, True), back.at[it, c], scans, emit)

        @pl.when(it < ITERS - 1)
        def _():
            start_halo(0, it + 1, c)

        @pl.when(it == ITERS - 1)
        def _():
            start_both(swap_out(c))

    steps = (forward_scans, forward_frames, back_frames, back_scans)
    total_steps = len(steps) * ITERS
    arrive(0)

    def wave(t, carry):
        def tile(c, inner):
            stage = t - c
            live = jnp.logical_and(stage >= 0, stage < total_steps)
            for n, step in enumerate(steps):

                @pl.when(jnp.logical_and(live, lax.rem(stage + total_steps, len(steps)) == n))
                def _(step=step):
                    step(stage // len(steps), c)

            return inner

        lax.fori_loop(0, tiles, tile, 0)

        @pl.when(t + 1 < tiles)
        def _():
            arrive(t + 1)

        return carry

    lax.fori_loop(0, total_steps + tiles - 1, wave, 0)

    def finish(c, carry):
        away, own = swap_out(c)
        own.wait()
        away.wait()
        swap_in_remote(c).wait_send()
        return carry

    lax.fori_loop(0, tiles, finish, 0)

    def sent(index, carry):
        it, c = index // tiles, lax.rem(index, tiles)
        for kind in range(len(fields)):
            on_halo(kind, it, c, lambda copy: copy.wait_send(), False)
        return carry

    lax.fori_loop(0, ITERS * tiles, sent, 0)


def deblur(observed, frame_kernel, scan_kernel):
    frames, scans, channels = observed.shape
    tiles = channels // 2 // LANES
    radius = (frame_kernel.shape[0] - 1) // 2
    sizes = lax.axis_size("rt"), lax.axis_size("mob")
    tall = (2 * frames, scans + 2 * SUB, LANES)
    long = (2 * frames + 2 * radius, scans, LANES)
    smem = pl.BlockSpec(memory_space=pltpu.SMEM)
    anywhere = pl.BlockSpec(memory_space=pl.ANY)
    dma = pltpu.SemaphoreType.DMA
    return pl.pallas_call(
        functools.partial(deblur_body, sizes),
        in_specs=[smem, smem, anywhere],
        out_specs=anywhere,
        out_shape=jax.ShapeDtypeStruct(observed.shape, jnp.float32),
        scratch_shapes=[
            pltpu.VMEM((ITERS + 1, tiles) + tall, jnp.float32),
            pltpu.VMEM((ITERS, tiles) + long, jnp.float32),
            pltpu.VMEM((ITERS, tiles) + long, jnp.float32),
            pltpu.VMEM((ITERS, tiles) + tall, jnp.float32),
            dma((4, ITERS, tiles, 2)),
            dma((4, ITERS, tiles, 2)),
            dma((2, tiles)),
            dma((2, tiles)),
            dma((2, tiles)),
        ],
        compiler_params=pltpu.CompilerParams(
            collective_id=2, has_side_effects=True, vmem_limit_bytes=50 * 1024 * 1024
        ),
        cost_estimate=pl.CostEstimate(
            flops=4 * ITERS * (frame_kernel.shape[0] + scan_kernel.shape[0]) * observed.size,
            bytes_accessed=8 * observed.size,
            transcendentals=0,
        ),
    )(frame_kernel, scan_kernel, observed)


def partner(axis, bit):
    return lax.bitwise_xor(lax.axis_index(axis), bit)


def bits_of(size):
    return [1 << n for n in range(size.bit_length() - 1)]


def greet(stages):
    barrier = pltpu.get_barrier_semaphore()
    for axis, bit in stages:
        pl.semaphore_signal(
            barrier,
            inc=1,
            device_id={axis: partner(axis, bit)},
            device_id_type=pl.DeviceIdType.MESH,
        )
    pl.semaphore_wait(barrier, len(stages))


def exchange(src, dst, send_sem, recv_sem, stage):
    axis, bit = stage
    copy = pltpu.make_async_remote_copy(
        src_ref=src,
        dst_ref=dst,
        send_sem=send_sem,
        recv_sem=recv_sem,
        device_id={axis: partner(axis, bit)},
        device_id_type=pl.DeviceIdType.MESH,
    )
    copy.start()
    return copy


def correlate_body(stages, groups, cells, est_ref, prow_ref, fcol_ref, out_ref, *scratch):
    count = len(stages)
    sums, got, sum_send, sum_recv, send_sem, recv_sem = scratch[:6]
    held = scratch[6 : 6 + count]
    landed = scratch[6 + count :]
    mobs, rows_of = groups
    prec = est_ref.shape[1] - mobs * out_ref.shape[1]
    rows, columns = out_ref.shape
    part = columns // CHUNKS
    peers = [("mob", n) for n in range(1, mobs)] + [("rt", n) for n in range(1, rows_of)]
    greet(peers)
    here = jnp.sum(est_ref[...], axis=0, keepdims=True)
    lane_tiles = est_ref.shape[1] // LANES
    sums[0] = jnp.zeros(sums.shape[1:], jnp.float32)
    for k in range(lane_tiles):
        sums[0, k : k + 1, :] = here[:, k * LANES : (k + 1) * LANES]
    for n, axis in enumerate(("mob", "rt")):
        slots = [i for i, peer in enumerate(peers) if peer[0] == axis]
        flying = [
            exchange(sums.at[n], got.at[i], sum_send.at[i], sum_recv.at[i], peers[i])
            for i in slots
        ]
        total = sums[n]
        for i, copy in zip(slots, flying):
            copy.wait()
            total = total + got[i]
        sums[n + 1] = total
    mean = jnp.concatenate([sums[2, k : k + 1, :] for k in range(lane_tiles)], axis=1) / cells
    left = (est_ref[:, :prec] - mean[:, :prec]).astype(jnp.bfloat16)
    wide = left.astype(jnp.float32)
    left_squares = jnp.sum(wide * wide, axis=0, keepdims=True)
    across = left.T
    first = held[0]
    upper = lax.broadcasted_iota(jnp.int32, (SUB, columns), 0) < SUB // 2
    for m in range(mobs):
        start = prec + m * columns
        right = (
            est_ref[:, start : start + columns] - mean[:, start : start + columns]
        ).astype(jnp.bfloat16)
        wide = right.astype(jnp.float32)
        right_squares = jnp.sum(wide * wide, axis=0, keepdims=True)
        squares = jnp.where(upper, right_squares, left_squares)
        product = jnp.dot(across, right, preferred_element_type=jnp.float32)
        for r in range(rows_of):
            for k in range(CHUNKS):
                block = first.at[k, m // 2, m % 2, r]
                block[:rows, :] = product[r * rows : (r + 1) * rows, k * part : (k + 1) * part]
                block[rows:, :] = squares[:, k * part : (k + 1) * part]

    def send_chunk(n, k):
        axis, bit = stages[n]
        mine = lax.rem(lax.axis_index(axis) // bit, 2)
        return exchange(
            held[n].at[k, :, 1 - mine],
            landed[n].at[k],
            send_sem.at[n, k],
            recv_sem.at[n, k],
            stages[n],
        )

    copies = [send_chunk(0, k) for k in range(CHUNKS)]
    totals = [None] * CHUNKS
    for n, (axis, bit) in enumerate(stages):
        mine = lax.rem(lax.axis_index(axis) // bit, 2)
        for k in range(CHUNKS):
            copies[k].wait()
            for i in range(held[n].shape[1]):
                total = held[n][k, i, mine] + landed[n][k, i]
                if n + 1 == count:
                    totals[k] = total
                elif stages[n + 1][0] == axis:
                    held[n + 1][k, i // 2, i % 2] = total
                else:
                    for r in range(rows_of):
                        held[n + 1][k, r // 2, r % 2] = total[r]
            if n + 1 < count:
                copies[k] = send_chunk(n + 1, k)
    total = jnp.concatenate(totals, axis=1)
    column = 1.0 / jnp.sqrt(total[rows : rows + 1, :] + 1e-06)
    row = 1.0 / jnp.sqrt(total[rows + SUB // 2 : rows + SUB // 2 + 1, :] + 1e-06)
    place = lax.broadcasted_iota(jnp.int32, (rows, prec), 1)
    wanted = lax.broadcasted_iota(jnp.int32, (rows, prec), 0) + lax.axis_index("rt") * rows
    row = jnp.sum(jnp.where(place == wanted, row, 0.0), axis=1, keepdims=True)
    same = (prow_ref[...] == fcol_ref[...]).astype(jnp.float32)
    out_ref[...] = same * total[:rows, :] * row * column


def correlate(estimate, prec_window, frag_window):
    frames, scans, channels = estimate.shape
    mobs, rows_of = lax.axis_size("mob"), lax.axis_size("rt")
    rows, columns = prec_window.shape[0], frag_window.shape[0]
    stages = [("mob", bit) for bit in bits_of(mobs)] + [("rt", bit) for bit in bits_of(rows_of)]
    count = len(stages)
    peers = mobs + rows_of - 2
    tile = (rows + SUB, columns // CHUNKS)
    sum_rows = -(-channels // (LANES * SUB)) * SUB
    held, landed = [], []
    for axis, bit in stages:
        if axis == "mob":
            span, tail = mobs // (2 * bit), (rows_of,) + tile
        else:
            span, tail = rows_of // (2 * bit), tile
        held.append(pltpu.VMEM((CHUNKS, span, 2) + tail, jnp.float32))
        landed.append(pltpu.VMEM((CHUNKS, span) + tail, jnp.float32))
    whole = pl.BlockSpec(memory_space=pltpu.VMEM)
    cells = frames * scans * mobs * rows_of
    return pl.pallas_call(
        functools.partial(correlate_body, stages, (mobs, rows_of), cells),
        in_specs=[whole] * 3,
        out_specs=whole,
        out_shape=jax.ShapeDtypeStruct((rows, columns), jnp.float32),
        scratch_shapes=[
            pltpu.VMEM((3, sum_rows, LANES), jnp.float32),
            pltpu.VMEM((peers, sum_rows, LANES), jnp.float32),
            pltpu.SemaphoreType.DMA((peers,)),
            pltpu.SemaphoreType.DMA((peers,)),
            pltpu.SemaphoreType.DMA((count, CHUNKS)),
            pltpu.SemaphoreType.DMA((count, CHUNKS)),
        ]
        + held
        + landed,
        compiler_params=pltpu.CompilerParams(
            collective_id=1, has_side_effects=True, vmem_limit_bytes=40 * 1024 * 1024
        ),
        cost_estimate=pl.CostEstimate(
            flops=2 * frames * scans * PREC * (channels - PREC),
            bytes_accessed=4 * frames * scans * channels,
            transcendentals=0,
        ),
    )(
        estimate.reshape(frames * scans, channels),
        prec_window.reshape(rows, 1),
        frag_window.reshape(1, columns),
    )


def local(observed, frame_kernel, scan_kernel, prec_window, frag_window):
    estimate = deblur(observed, frame_kernel, scan_kernel)
    return (estimate, correlate(estimate, prec_window, frag_window))


def solution(mesh):
    placed = (P("rt", "mob", None), P(), P(), P("rt"), P("mob"))
    return jax.shard_map(
        local,
        mesh=mesh,
        in_specs=placed,
        out_specs=(P("rt", "mob", None), P("rt", "mob")),
        check_vma=False,
    )
```
